128 devices in a mesh: branch: 2 (over x_lo), row: 4 (over z), col: 16 (over x_hi, y, core).
Axes of the slice: x: 4 (x_hi: 2, x_lo: 2; x = x_hi * 2 + x_lo), y: 4, z: 4, core: 2. Of those that a mesh axis runs over, the one named last changes fastest.
Arguments:
- x_act: bfloat16 [2, 1024, 5120], P('branch', 'row', 'col'), may hold values from -6 to 6
- grad_out: bfloat16 [2, 1024, 5120], P('branch', 'row', 'col'), may hold values from -6 to 6
- w_gate: bfloat16 [5120, 8192], P('row', 'col'), may hold values from -0.078125 to 0.078125
- w_up: bfloat16 [5120, 8192], P('row', 'col'), may hold values from -0.078125 to 0.078125
- w_down: bfloat16 [8192, 5120], P('col', 'row'), may hold values from -0.0625 to 0.0625
Outputs:
- out_act: bfloat16 [2, 1024, 5120], P('branch', 'row', 'col')
- grad_in: bfloat16 [2, 1024, 5120], P('branch', 'row', 'col')
- grad_gate: float32 [5120, 8192], P('row', 'col')
- grad_up: float32 [5120, 8192], P('row', 'col')
- grad_down: float32 [8192, 5120], P('col', 'row')
The draws below stay inside these ranges and needn't reach their ends.
All inputs are finite; a program needn't handle non-finite values.
Results may differ from the reference program's by a relative error of at most 0.019.
Values may be sent and summed in bfloat16 or wider, within the bound.
A program may use at most 128 MiB of HBM per device.

```python
import jax
import jax.numpy as jnp
from jax import lax

D = 5120
FF = 8192
TOK_DEV = 256
TOKENS = 1024
PASSES = 2
N_BRANCH = 2
N_ROW = 4


def block_levels(stream_key, dims, pieces, smallest, top_value):
    level = 1.0
    for position, shards_of in pieces:
        steps = jax.random.uniform(jax.random.fold_in(jax.random.fold_in(stream_key, 6), position), (shards_of,), jnp.float32, smallest / len(pieces), top_value / len(pieces))
        level = level * jnp.repeat(jnp.exp(steps), dims[position] // shards_of).reshape((-1,) + (1,) * (len(dims) - 1 - position))
    return level


def normal_values(stream_key, shape, scale, limit, pieces=(), dtype=jnp.bfloat16):
    level = block_levels(stream_key, shape, pieces, -0.22, 0.18) if pieces else 1.0
    drawn = jax.random.normal(stream_key, shape, jnp.float32) * scale * level
    return jnp.minimum(jnp.maximum(drawn, -limit), limit).astype(dtype)


def setup_inputs(seed: int = 0) -> dict:
    seeds = jax.random.split(jax.random.key(seed), 6)
    x_act = normal_values(seeds[0], (PASSES, TOKENS, D), 1.0, 6.0, ((0, 2), (1, 4), (2, 16)))
    grad_out = normal_values(seeds[1], (PASSES, TOKENS, D), 1.0, 6.0, ((0, 2), (1, 4), (2, 16)))
    w_gate = normal_values(seeds[2], (D, FF), D ** -0.5, 0.078125, ((0, 4), (1, 16)))
    w_up = normal_values(seeds[3], (D, FF), D ** -0.5, 0.078125, ((0, 4), (1, 16)))
    w_down = normal_values(seeds[4], (FF, D), FF ** -0.5, 0.0625, ((0, 16), (1, 4)))
    return dict(x_act=x_act, grad_out=grad_out, w_gate=w_gate, w_up=w_up, w_down=w_down)


def rounded(value):
    low = lax.optimization_barrier(value.astype(jnp.bfloat16))
    return low.astype(jnp.float32)


def reference(x_act, grad_out, w_gate, w_up, w_down):
    blocks_x = x_act.reshape(N_BRANCH * N_ROW, TOK_DEV, D)
    blocks_dy = grad_out.reshape(N_BRANCH * N_ROW, TOK_DEV, D)

    def step(carry, pair):
        tok_rows, dy_rows = pair
        gate = jnp.dot(tok_rows, w_gate, preferred_element_type=jnp.float32)
        up = jnp.dot(tok_rows, w_up, preferred_element_type=jnp.float32)
        sig = jax.nn.sigmoid(gate)
        swish = gate * sig
        hidden = (swish * up).astype(jnp.bfloat16)
        out_rows = jnp.dot(hidden, w_down, preferred_element_type=jnp.float32).astype(jnp.bfloat16)
        d_hidden = jnp.dot(dy_rows, w_down.T, preferred_element_type=jnp.float32)
        d_gate = (d_hidden * up * sig * (1.0 + gate * (1.0 - sig))).astype(jnp.bfloat16)
        d_up = (d_hidden * swish).astype(jnp.bfloat16)
        dx_rows = (jnp.dot(d_gate, w_gate.T, preferred_element_type=jnp.float32)
                   + jnp.dot(d_up, w_up.T, preferred_element_type=jnp.float32)).astype(jnp.bfloat16)
        acc_gate = carry[0] + rounded(jnp.dot(tok_rows.T, d_gate, preferred_element_type=jnp.float32))
        acc_up = carry[1] + rounded(jnp.dot(tok_rows.T, d_up, preferred_element_type=jnp.float32))
        acc_down = carry[2] + rounded(jnp.dot(hidden.T, dy_rows, preferred_element_type=jnp.float32))
        return (acc_gate, acc_up, acc_down), (out_rows, dx_rows)

    start = (jnp.zeros((D, FF), jnp.float32), jnp.zeros((D, FF), jnp.float32), jnp.zeros((FF, D), jnp.float32))
    totals, outs = lax.scan(step, start, (blocks_x, blocks_dy))
    out_act = outs[0].reshape(N_BRANCH, TOKENS, D)
    grad_in = outs[1].reshape(N_BRANCH, TOKENS, D)
    return (out_act, grad_in, totals[0], totals[1], totals[2])
```

```python
import functools

import jax
import jax.numpy as jnp
from jax import lax
from jax.experimental import pallas as pl
from jax.experimental.pallas import tpu as pltpu
from jax.sharding import PartitionSpec as P

MESH = pl.DeviceIdType.MESH
BF16 = jnp.bfloat16
F32 = jnp.float32

N_ROW = 4
FEAT = 320
TOK = 256
PANEL = 1280
HID = 512
NQ = 4
HC = HID // NQ


def dot_nn(left, right):
    return jnp.dot(left, right, preferred_element_type=F32)


def dot_nt(left, right):
    return lax.dot_general(left, right, (((1,), (1,)), ((), ())), preferred_element_type=F32)


def layer_kernel(
    x_in, dy_in, wg, wu, wd,
    out_t, dx_t, own_gu, got_gu, own_dn, got_dn,
    xs, wgut, wdt,
    p_gu, r_gu, o_gu, p_dh, r_dh, o_dh, c_gate, c_up,
    hid, dgu, g_gu, g_dn,
    o_part, o_sib, o_sum, o_y, o_fin, o_got,
    p0_s, p0_r, p1_s, p1_r, p2_s, p2_r,
    gu_s, gu_r, hb_s, hb_r, dh_s, dh_r, dg_s, dg_r,
    xd_s, xd_r, xg_s, xg_r, loc_d, loc_g,
    sb_s, sb_r, yr_s, yr_r, fn_s, fn_r,
):
    b, z, c = lax.axis_index("branch"), lax.axis_index("row"), lax.axis_index("col")
    y, xh, sub, core = (c // 2) % 4, c // 8, c % 4, c % 2
    yh = y // 2
    home = c // 4 == z

    def at_z(d):
        return (b, (z + d) % N_ROW, c)

    def at_y(d):
        return (b, z, xh * 8 + ((y + d) % 4) * 2 + core)

    sibling = (b, z, c + 1 - 2 * core)
    partner = (1 - b, z, c)

    def spread_to(h):
        return (b, c // 4, h * 8 + (z % 2) * 4 + sub)

    def spread_from(i):
        return (b, 2 * i + yh, 4 * z + sub)

    def rows_of(j):
        return pl.ds(pl.multiple_of(j * FEAT, 64), FEAT)

    def remote(src, dst, ssem, rsem, to):
        return pltpu.make_async_remote_copy(
            src_ref=src, dst_ref=dst, send_sem=ssem, recv_sem=rsem, device_id=to, device_id_type=MESH
        )

    barrier = pltpu.get_barrier_semaphore()
    for to in [at_z(1), at_z(2), at_z(3), at_y(1), at_y(2), at_y(3), sibling, partner]:
        pl.semaphore_signal(barrier, inc=1, device_id=to, device_id_type=MESH)
    for i in range(2):
        @pl.when(jnp.logical_not(home & (xh == i)))
        def _(i=i):
            pl.semaphore_signal(barrier, inc=1, device_id=spread_to(i), device_id_type=MESH)
            pl.semaphore_signal(barrier, inc=1, device_id=spread_from(i), device_id_type=MESH)

    pl.semaphore_wait(barrier, jnp.where(home, 10, 12))

    acts = (x_in, dy_in)

    def spread_copy(s, h):
        return remote(
            acts[s], xs.at[s, z // 2, z % 2, rows_of(sub)], p0_s.at[s, h], p0_r.at[s, z // 2], spread_to(h)
        )

    def spread_local(s):
        return pltpu.make_async_copy(
            acts[s], xs.at[s, z // 2, z % 2, rows_of(sub)], p0_r.at[s, z // 2]
        )

    def spread_start(s):
        for h in range(2):
            @pl.when(jnp.logical_not(home & (xh == h)))
            def _(h=h):
                spread_copy(s, h).start()

        @pl.when(home)
        def _():
            spread_local(s).start()

    def spread_wait_recv(s):
        for i in range(2):
            pltpu.make_async_copy(
                acts[s], xs.at[s, i, yh, rows_of(sub)], p0_r.at[s, i]
            ).wait()

    def spread_wait_send(s):
        for h in range(2):
            @pl.when(jnp.logical_not(home & (xh == h)))
            def _(h=h):
                spread_copy(s, h).wait_send()

    def group(s, d):
        yy = (y - d + 4) % 4
        return xs.at[s, :, yy // 2, rows_of(2 * (yy % 2) + core)]

    def y_copy(s, d):
        return remote(group(s, 0), group(s, 0), p1_s.at[s, d - 1], p1_r.at[s, d - 1], at_y(d))

    def y_wait_recv(s, d):
        remote(group(s, 0), group(s, d), p1_s.at[s, d - 1], p1_r.at[s, d - 1], at_y(d)).wait_recv()

    def sib_copy(s, d):
        return remote(group(s, d), group(s, d), p2_s.at[s, d], p2_r.at[s, d], sibling)

    def sib_wait_recv(s):
        for d in range(4):
            yy = (y - d + 4) % 4
            there = xs.at[s, :, yy // 2, rows_of(2 * (yy % 2) + 1 - core)]
            remote(group(s, d), there, p2_s.at[s, d], p2_r.at[s, d], sibling).wait_recv()

    def gather_start(s):
        for d in (2, 1, 3):
            y_copy(s, d).start()
        sib_copy(s, 0).start()

    def gather_forward(s):
        for d in (1, 3, 2):
            y_wait_recv(s, d)
            sib_copy(s, d).start()

    spread_start(0)
    spread_start(1)

    @pl.loop(0, NQ)
    def _(q):
        cols = pl.ds(pl.multiple_of(q * HC, HC), HC)
        wgut[pl.ds(pl.multiple_of(q * 2 * HC, HC), HC), :] = wg[:, cols].T
        wgut[pl.ds(pl.multiple_of(q * 2 * HC + HC, HC), HC), :] = wu[:, cols].T

    spread_wait_recv(0)
    gather_start(0)

    @pl.loop(0, NQ)
    def _(q):
        cols = pl.ds(pl.multiple_of(q * HC, HC), HC)
        wdt[:, cols] = wd[cols, :].T

    spread_wait_recv(1)
    for d in (2, 1, 3):
        y_copy(0, d).wait_send()
    gather_start(1)
    gather_forward(0)
    sib_wait_recv(0)

    def z_loop(q, lhs, s, parts, own, send, recv, remote_dst):
        @pl.loop(0, 3)
        def _(i):
            t = (z + i + 1) % 4
            parts[q, i] = dot_nn(lhs(), xs[s, t // 2, t % 2]).astype(BF16)
            remote(parts.at[q, i], remote_dst.at[q, i], send.at[q, i], recv.at[q, i], at_z(i + 1)).start()

        own[q] = dot_nn(lhs(), xs[s, z // 2, z % 2])

    def z_sum(q, s, parts, own, send, recv, remote_dst):
        total = own[q]
        for i in range(3):
            remote(parts.at[q, i], remote_dst.at[q, i], send.at[q, i], recv.at[q, i], at_z(i + 1)).wait_recv()
        for i in range(3):
            total = total + remote_dst[q, i].astype(F32)
        return total

    gu_args = (0, p_gu, o_gu, gu_s, gu_r, r_gu)
    dh_args = (1, p_dh, o_dh, dh_s, dh_r, r_dh)

    def gate_up(q):
        z_loop(q, lambda: wgut[q * 2 * HC:(q + 1) * 2 * HC, :], *gu_args)

    def d_hidden(q):
        z_loop(q, lambda: wd[q * HC:(q + 1) * HC, :], *dh_args)

    def hid_copy(q, i, t):
        piece = hid.at[t, q * HC:(q + 1) * HC]
        return remote(piece, piece, hb_s.at[q, i], hb_r.at[q, i], at_z(i + 1))

    def dgu_copy(q, i, t):
        piece = dgu.at[t, :, q * HC:(q + 1) * HC]
        return remote(piece, piece, dg_s.at[q, i], dg_r.at[q, i], at_z(i + 1))

    def hidden_step(q):
        total = z_sum(q, *gu_args)
        gate, up = total[:HC], total[HC:]
        sig = jax.nn.sigmoid(gate)
        swish = gate * sig
        hid[z, q * HC:(q + 1) * HC] = (swish * up).astype(BF16)
        for i in (1, 0, 2):
            hid_copy(q, i, z).start()
        c_gate[q] = up * sig * (1.0 + gate * (1.0 - sig))
        c_up[q] = swish

    def d_step(q):
        dh = z_sum(q, *dh_args)
        dgu[z, 0, q * HC:(q + 1) * HC] = (dh * c_gate[q]).astype(BF16)
        dgu[z, 1, q * HC:(q + 1) * HC] = (dh * c_up[q]).astype(BF16)
        for i in (1, 0, 2):
            dgu_copy(q, i, z).start()

    def down_copy(q):
        return remote(g_dn.at[q], got_dn.at[q], xd_s.at[q], xd_r.at[q], partner)

    def gu_copy(q):
        return remote(g_gu.at[q], got_gu.at[q], xg_s.at[q], xg_r.at[q], partner)

    def down_local(q):
        return pltpu.make_async_copy(g_dn.at[q], own_dn.at[q], loc_d.at[q])

    def gu_local(q):
        return pltpu.make_async_copy(g_gu.at[q], own_gu.at[q], loc_g.at[q])

    def grad_down(q):
        for i in range(3):
            hid_copy(q, i, (z + 3 - i) % 4).wait_recv()

        @pl.loop(0, 2)
        def _(m):
            feats = pl.ds(pl.multiple_of(m * 640, 640), 640)
            total = None
            for t in range(4):
                part = dot_nt(hid[t, q * HC:(q + 1) * HC], xs[1, t // 2, t % 2, feats])
                total = part if total is None else total + part
            g_dn[q, :, feats] = total.astype(BF16)

        down_copy(q).start()
        down_local(q).start()

    def dgu_wait(q):
        for i in range(3):
            dgu_copy(q, i, (z + 3 - i) % 4).wait_recv()

    def grad_gate_up(q):
        @pl.loop(0, 2)
        def _(m):
            feats = pl.ds(pl.multiple_of(m * 640, 640), 640)
            total = None
            for t in range(4):
                both = jnp.concatenate(
                    [dgu[t, 0, q * HC:(q + 1) * HC], dgu[t, 1, q * HC:(q + 1) * HC]], axis=0
                )
                part = dot_nt(xs[0, t // 2, t % 2, feats], both)
                total = part if total is None else total + part
            g_gu[q, feats, :] = total.astype(BF16)

        gu_copy(q).start()
        gu_local(q).start()

    def sum_sib(s, h):
        there = rows_of(2 * h + 1 - core)
        return remote(o_part.at[s, :, :, there], o_sib.at[s, h], sb_s.at[s, h], sb_r.at[s, h], sibling)

    def sum_terms(s, h, who, product):
        rows = rows_of(2 * h + who)

        @pl.loop(0, 4)
        def _(t):
            o_part[s, t // 2, t % 2, rows, :] = product(rows, t).astype(BF16)

    def sum_start(s, product):
        for h in range(2):
            sum_terms(s, h, 1 - core, product)
            sum_sib(s, h).start()
        for h in range(2):
            sum_terms(s, h, core, product)

    def sum_y(s, d):
        return remote(o_sum.at[s, d], o_y.at[s, d - 1], yr_s.at[s, d - 1], yr_r.at[s, d - 1], at_y(d))

    def sum_cores(s):
        for h in range(2):
            sum_sib(s, h).wait_recv()
        for d in (2, 1, 3, 0):
            yy = (y + d) % 4
            for i in range(2):
                mine = o_part[s, i, yy // 2, rows_of(2 * (yy % 2) + core), :].astype(F32)
                o_sum[s, d, i] = (mine + o_sib[s, yy % 2, i, yy // 2].astype(F32)).astype(BF16)
            if d:
                sum_y(s, d).start()

    def sum_final(s, i):
        return remote(o_fin.at[s, i], o_got.at[s, xh], fn_s.at[s, i], fn_r.at[s, xh], spread_from(i))

    def sum_chips(s):
        for d in (1, 3, 2):
            sum_y(s, d).wait_recv()
        for i in range(2):
            total = o_sum[s, 0, i].astype(F32)
            for d in range(3):
                total = total + o_y[s, d, i].astype(F32)
            o_fin[s, i] = total.astype(BF16)

            @pl.when(jnp.logical_not(home & (xh == i)))
            def _(i=i):
                sum_final(s, i).start()

            @pl.when(home & (xh == i))
            def _(i=i):
                pltpu.make_async_copy(o_fin.at[s, i], o_got.at[s, xh], fn_r.at[s, xh]).start()

    def sum_end(s, result):
        for h in range(2):
            pltpu.make_async_copy(o_fin.at[s, h], o_got.at[s, h], fn_r.at[s, h]).wait()
        result[...] = (o_got[s, 0].astype(F32) + o_got[s, 1].astype(F32)).astype(BF16)

    gate_up(0)
    gate_up(1)
    gather_forward(1)
    hidden_step(0)
    gate_up(2)
    hidden_step(1)
    sib_wait_recv(1)
    grad_down(0)
    gate_up(3)
    d_hidden(0)
    hidden_step(2)
    grad_down(1)
    d_hidden(1)
    hidden_step(3)
    d_step(0)
    grad_down(2)
    d_hidden(2)
    d_step(1)
    d_hidden(3)
    grad_down(3)
    d_step(2)
    dgu_wait(0)
    grad_gate_up(0)
    d_step(3)
    sum_start(0, lambda rows, t: dot_nn(wdt[rows, :], hid[t]))
    dgu_wait(1)
    grad_gate_up(1)
    sum_cores(0)
    dgu_wait(2)
    grad_gate_up(2)
    dgu_wait(3)
    sum_start(1, lambda rows, t: dot_nn(wg[rows, :], dgu[t, 0]) + dot_nn(wu[rows, :], dgu[t, 1]))
    sum_chips(0)
    sum_cores(1)
    grad_gate_up(3)
    sum_end(0, out_t)
    sum_chips(1)
    sum_end(1, dx_t)

    for q in range(NQ):
        for i in range(3):
            remote(p_gu.at[q, i], r_gu.at[q, i], gu_s.at[q, i], gu_r.at[q, i], at_z(i + 1)).wait_send()
            remote(p_dh.at[q, i], r_dh.at[q, i], dh_s.at[q, i], dh_r.at[q, i], at_z(i + 1)).wait_send()
            hid_copy(q, i, z).wait_send()
            dgu_copy(q, i, z).wait_send()
    for s in range(2):
        spread_wait_send(s)
        for d in range(4):
            sib_copy(s, d).wait_send()
        for d in range(1, 4):
            if s == 1:
                y_copy(s, d).wait_send()
            sum_y(s, d).wait_send()
        for i in range(2):
            sum_sib(s, i).wait_send()

            @pl.when(jnp.logical_not(home & (xh == i)))
            def _(s=s, i=i):
                sum_final(s, i).wait_send()

    for q in range(NQ):
        down_local(q).wait()
        gu_local(q).wait()
        down_copy(q).wait()
        gu_copy(q).wait()


def add_kernel(own_gu, got_gu, own_dn, got_dn, gate, up, down):
    total = own_gu[0].astype(F32) + got_gu[0].astype(F32)
    gate[...] = total[:, :HC]
    up[...] = total[:, HC:]
    down[...] = own_dn[0].astype(F32) + got_dn[0].astype(F32)


def body(x_act, grad_out, w_gate, w_up, w_down):
    vmem = pl.BlockSpec(memory_space=pltpu.VMEM)
    hbm = pl.BlockSpec(memory_space=pl.ANY)
    dma = pltpu.SemaphoreType.DMA
    shape = jax.ShapeDtypeStruct

    def buf(*dims, dtype=BF16):
        return pltpu.VMEM(dims, dtype)

    outs = pl.pallas_call(
        layer_kernel,
        out_shape=[
            shape((FEAT, TOK), BF16), shape((FEAT, TOK), BF16),
            shape((NQ, PANEL, 2 * HC), BF16), shape((NQ, PANEL, 2 * HC), BF16),
            shape((NQ, HC, PANEL), BF16), shape((NQ, HC, PANEL), BF16),
        ],
        in_specs=[vmem] * 5,
        out_specs=[vmem, vmem, hbm, hbm, hbm, hbm],
        scratch_shapes=[
            buf(2, 2, 2, PANEL, TOK), buf(2 * HID, PANEL), buf(PANEL, HID),
            buf(NQ, 3, 2 * HC, TOK), buf(NQ, 3, 2 * HC, TOK), buf(NQ, 2 * HC, TOK, dtype=F32),
            buf(NQ, 3, HC, TOK), buf(NQ, 3, HC, TOK), buf(NQ, HC, TOK, dtype=F32),
            buf(NQ, HC, TOK, dtype=F32), buf(NQ, HC, TOK, dtype=F32),
            buf(4, HID, TOK), buf(4, 2, HID, TOK), buf(NQ, PANEL, 2 * HC), buf(NQ, HC, PANEL),
            buf(2, 2, 2, PANEL, TOK), buf(2, 2, 2, 2, FEAT, TOK), buf(2, 4, 2, FEAT, TOK),
            buf(2, 3, 2, FEAT, TOK), buf(2, 2, FEAT, TOK), buf(2, 2, FEAT, TOK),
            dma((2, 2)), dma((2, 2)), dma((2, 3)), dma((2, 3)), dma((2, 4)), dma((2, 4)),
            dma((NQ, 3)), dma((NQ, 3)), dma((NQ, 3)), dma((NQ, 3)),
            dma((NQ, 3)), dma((NQ, 3)), dma((NQ, 3)), dma((NQ, 3)),
            dma((NQ,)), dma((NQ,)), dma((NQ,)), dma((NQ,)), dma((NQ,)), dma((NQ,)),
            dma((2, 2)), dma((2, 2)), dma((2, 3)), dma((2, 3)), dma((2, 2)), dma((2, 2)),
        ],
        name="layer",
        compiler_params=pltpu.CompilerParams(
            collective_id=0, has_side_effects=True, vmem_limit_bytes=60 * 2**20
        ),
    )(x_act[0].T, grad_out[0].T, w_gate, w_up, w_down)
    out_t, dx_t, own_gu, got_gu, own_dn, got_dn = outs

    gu_block = pl.BlockSpec((1, PANEL, 2 * HC), lambda q: (q, 0, 0))
    dn_block = pl.BlockSpec((1, HC, PANEL), lambda q: (q, 0, 0))
    grads = pl.pallas_call(
        add_kernel,
        grid=(NQ,),
        out_shape=[shape((PANEL, HID), F32), shape((PANEL, HID), F32), shape((HID, PANEL), F32)],
        in_specs=[gu_block, gu_block, dn_block, dn_block],
        out_specs=[
            pl.BlockSpec((PANEL, HC), lambda q: (0, q)),
            pl.BlockSpec((PANEL, HC), lambda q: (0, q)),
            pl.BlockSpec((HC, PANEL), lambda q: (q, 0)),
        ],
        name="add_passes",
        compiler_params=pltpu.CompilerParams(vmem_limit_bytes=32 * 2**20),
    )(own_gu, got_gu, own_dn, got_dn)
    return (out_t.T[None], dx_t.T[None], *grads)


def solution(mesh):
    acts = P("branch", "row", "col")
    return jax.shard_map(
        body,
        mesh=mesh,
        in_specs=(acts, acts, P("row", "col"), P("row", "col"), P("col", "row")),
        out_specs=(acts, acts, P("row", "col"), P("row", "col"), P("col", "row")),
        check_vma=False,
    )
```

```python
import functools

import jax
import jax.numpy as jnp
from jax import lax
from jax.experimental import pallas as pl
from jax.experimental.pallas import tpu as pltpu
from jax.sharding import PartitionSpec as P

MESH = pl.DeviceIdType.MESH
BF16 = jnp.bfloat16
F32 = jnp.float32

N_ROW = 4
FEAT = 320
TOK = 256
PANEL = 1280
HID = 512
NQ = 4
HC = HID // NQ


def dot_nn(left, right):
    return jnp.dot(left, right, preferred_element_type=F32)


def dot_nt(left, right):
    return lax.dot_general(left, right, (((1,), (1,)), ((), ())), preferred_element_type=F32)


def flip(a, b):
    return a + b - 2 * a * b


def layer_kernel(
    x_in, dy_in, wg_in, wu_in, wd_in,
    o_got, all_gu, all_dn,
    xs, wg, wu, wd, wgut, wdt,
    p_gu, t_gu, r_gu, o_gu, p_dh, t_dh, r_dh, o_dh, c_gate, c_up,
    hid, dgu, g_gu, g_dn, x_gu, x_dn,
    o_part, o_sib, o_sum, o_y, o_fin,
    w_r, wf_s, wf_r,
    p0_s, p0_r, p1_s, p1_r, p2_s, p2_r,
    gu_s, gu_r, hb_s, hb_r, dh_s, dh_r, dg_s, dg_r,
    xd_s, xd_r, xg_s, xg_r, loc_d, loc_g,
    sb_s, sb_r, yr_s, yr_r, fn_s, fn_r,
):
    b, z, c = lax.axis_index("branch"), lax.axis_index("row"), lax.axis_index("col")
    y, xh, sub, core = (c // 2) % 4, c // 8, c % 4, c % 2
    yh = y // 2
    zh, zl = z // 2, z % 2
    low = flip(yh, zl)

    def at_z(d):
        return (b, (z + d) % N_ROW, c)

    def at_y(d):
        return (b, z, xh * 8 + ((y + d) % 4) * 2 + core)

    sibling = (b, z, c + 1 - 2 * core)
    partner = (1 - b, z, c)
    other = (1 - b, z, (c + 8) % 16)

    def spread_to(h):
        return (b, c // 4, h * 8 + low * 4 + sub)

    def spread_from(i):
        return (b, 2 * i + low, 4 * z + sub)

    def to_self(h):
        return (c // 4 == z) & (xh == h) & (low == yh)

    def from_self(i):
        return (c // 4 == z) & (2 * i + low == z)

    def rows_of(j):
        return pl.ds(pl.multiple_of(j * FEAT, 64), FEAT)

    def remote(src, dst, ssem, rsem, to):
        return pltpu.make_async_remote_copy(
            src_ref=src, dst_ref=dst, send_sem=ssem, recv_sem=rsem, device_id=to, device_id_type=MESH
        )

    def weight_pair(i, n):
        part = pl.ds(pl.multiple_of(b * (HID // 2) + i * HC, HC), HC)
        mine, theirs = pl.ds((2 * i + 1) * HC, HC), pl.ds(2 * i * HC, HC)
        if n == 2:
            return wd_in.at[part], wd.at[mine], wd.at[theirs]
        src, dst = ((wg_in, wg), (wu_in, wu))[n]
        return src.at[:, part], dst.at[:, mine], dst.at[:, theirs]

    def weight_local(i, n):
        src, mine, _ = weight_pair(i, n)
        return pltpu.make_async_copy(src, mine, w_r.at[i, n])

    def weight_copy(i, n):
        src, _, theirs = weight_pair(i, n)
        return remote(src, theirs, wf_s.at[i, n], wf_r.at[i, n], other)

    for i in range(2):
        for n in range(3):
            weight_local(i, n).start()

    barrier = pltpu.get_barrier_semaphore()
    for to in [at_z(1), at_z(2), at_z(3), at_y(1), at_y(2), at_y(3), sibling, partner, other]:
        pl.semaphore_signal(barrier, inc=1, device_id=to, device_id_type=MESH)
    for i in range(2):
        @pl.when(jnp.logical_not(to_self(i)))
        def _(i=i):
            pl.semaphore_signal(barrier, inc=1, device_id=spread_to(i), device_id_type=MESH)

        @pl.when(jnp.logical_not(from_self(i)))
        def _(i=i):
            pl.semaphore_signal(barrier, inc=1, device_id=spread_from(i), device_id_type=MESH)

    stay = (c // 4 == z) & (low == yh)
    pl.semaphore_wait(barrier, jnp.where(stay, 11, 13))

    acts = (x_in, dy_in)

    def spread_copy(s, h):
        return remote(
            acts[s], xs.at[s, zh, zl, rows_of(sub)], p0_s.at[s, h], p0_r.at[s, zh], spread_to(h)
        )

    def spread_local(s):
        return pltpu.make_async_copy(
            acts[s], xs.at[s, zh, zl, rows_of(sub)], p0_r.at[s, zh]
        )

    def spread_start(s):
        for h in range(2):
            @pl.when(jnp.logical_not(to_self(h)))
            def _(h=h):
                spread_copy(s, h).start()

            @pl.when(to_self(h))
            def _():
                spread_local(s).start()

    def spread_wait_recv(s):
        for i in range(2):
            pltpu.make_async_copy(
                acts[s], xs.at[s, i, low, rows_of(sub)], p0_r.at[s, i]
            ).wait()

    def spread_wait_send(s):
        for h in range(2):
            @pl.when(jnp.logical_not(to_self(h)))
            def _(h=h):
                spread_copy(s, h).wait_send()

    def block(s, i, yy, k):
        return xs.at[s, i, flip(yy // 2, zl), rows_of(2 * (yy % 2) + k)]

    def group(s, d, k):
        yy = (y - d + 4) % 4
        return xs.at[s, :, flip(yy // 2, zl), rows_of(2 * (yy % 2) + k)]

    def y_copy(s, slot):
        if slot < 2:
            piece = group(s, 0, core)
        else:
            piece = block(s, slot - 2, (y + (3 if slot == 2 else 1)) % 4, core)
        to = at_y(1 if slot % 2 == 0 else 3)
        return remote(piece, piece, p1_s.at[s, slot], p1_r.at[s, slot], to)

    def y_wait_recv(s, slot):
        if slot < 2:
            piece = group(s, 1 if slot == 0 else 3, core)
        else:
            piece = block(s, slot - 2, (y + 2) % 4, core)
        remote(piece, piece, p1_s.at[s, slot], p1_r.at[s, slot], at_y(1)).wait_recv()

    def sib_copy(s, d):
        piece = group(s, d, core)
        return remote(piece, piece, p2_s.at[s, d], p2_r.at[s, d], sibling)

    def sib_wait_recv(s):
        for d in range(4):
            there = group(s, d, 1 - core)
            remote(there, there, p2_s.at[s, d], p2_r.at[s, d], sibling).wait_recv()

    def gather_start(s):
        y_copy(s, 0).start()
        y_copy(s, 1).start()
        sib_copy(s, 0).start()

    def gather_pass(s):
        y_wait_recv(s, 0)
        y_copy(s, 2).start()
        y_wait_recv(s, 1)
        y_copy(s, 3).start()
        sib_copy(s, 1).start()
        sib_copy(s, 3).start()

    def gather_last(s):
        y_wait_recv(s, 2)
        y_wait_recv(s, 3)
        sib_copy(s, 2).start()

    spread_start(0)

    for i, n in ((0, 0), (0, 1), (1, 0), (1, 1), (0, 2), (1, 2)):
        weight_copy(i, n).start()

    def turn(q):
        cols = pl.ds(q * HC, HC)
        wgut[q * 2 * HC:q * 2 * HC + HC, :] = wg[:, cols].T
        wgut[q * 2 * HC + HC:(q + 1) * 2 * HC, :] = wu[:, cols].T

    def turn_other(i):
        weight_copy(i, 0).wait_recv()
        weight_copy(i, 1).wait_recv()
        turn(2 * i)

    def turn_down():
        @pl.loop(0, NQ)
        def _(q):
            cols = pl.ds(pl.multiple_of(q * HC, HC), HC)
            wdt[:, cols] = wd[cols, :].T

    for i in range(2):
        for n in range(3):
            weight_local(i, n).wait()
        turn(2 * i + 1)

    spread_wait_recv(0)
    gather_start(0)
    spread_start(1)
    gather_pass(0)
    spread_wait_recv(1)
    gather_start(1)
    turn_other(0)
    gather_last(0)
    sib_wait_recv(0)

    def term_copy(flow, q, slot):
        _, parts, far, near, _, send, recv, half = flow
        rows = pl.ds((0, half, half, 0, 0, half)[slot], half)
        src = parts.at[q, (1, 1, 0, 2, 0, 2)[slot], rows]
        dst = far.at[q, slot] if slot < 2 else near.at[q, slot % 2, rows]
        return remote(src, dst, send.at[q, slot], recv.at[q, slot], at_z(3 if slot % 2 else 1))

    def terms(flow, q, lhs):
        s, parts, _, _, own, _, _, _ = flow
        for d in (2, 1, 3, 0):
            t = (z + d) % 4
            term = dot_nn(lhs, xs[s, t // 2, t % 2])
            if d == 0:
                own[q] = term
                continue
            parts[q, d - 1] = term.astype(BF16)
            for slot in {2: (0, 1), 1: (2,), 3: (3,)}[d]:
                term_copy(flow, q, slot).start()

    def relay(flow, q):
        _, parts, far, _, _, _, _, half = flow
        for slot in (0, 1):
            rows = pl.ds(slot * half, half)
            term_copy(flow, q, slot).wait_recv()
            parts[q, 2 * slot, rows, :] = (
                parts[q, 2 * slot, rows, :].astype(F32) + far[q, slot].astype(F32)
            ).astype(BF16)
            term_copy(flow, q, slot + 4).start()

    def total(flow, q):
        _, _, _, near, own, _, _, _ = flow
        for slot in (2, 3, 4, 5):
            term_copy(flow, q, slot).wait_recv()
        return own[q] + near[q, 0].astype(F32) + near[q, 1].astype(F32)

    gu_flow = (0, p_gu, t_gu, r_gu, o_gu, gu_s, gu_r, HC)
    dh_flow = (1, p_dh, t_dh, r_dh, o_dh, dh_s, dh_r, HC // 2)

    def gate_up(q):
        terms(gu_flow, q, wgut[q * 2 * HC:(q + 1) * 2 * HC, :])

    def d_hidden(q):
        terms(dh_flow, q, wd[q * HC:(q + 1) * HC, :])

    def hid_piece(q, t, half):
        if half is None:
            return hid.at[t, q * HC:(q + 1) * HC]
        return hid.at[t, q * HC + half * (HC // 2):q * HC + (half + 1) * (HC // 2)]

    def dgu_piece(q, t, half):
        rows = pl.ds(q * HC, HC)
        return dgu.at[t, :, rows] if half is None else dgu.at[t, half, rows]

    def block_copy(piece, q, slot, send, recv, step):
        part = piece(q, (z + (step, -step)[slot % 2] + 4) % 4, None if slot < 2 else slot - 2)
        return remote(part, part, send.at[q, slot], recv.at[q, slot], at_z(3 if slot % 2 else 1))

    def send_copy(flow, q, slot):
        piece, send, recv = flow
        return block_copy(piece, q, slot, send, recv, 0 if slot < 2 else 3)

    def recv_copy(flow, q, slot):
        piece, send, recv = flow
        return block_copy(piece, q, slot, send, recv, 3 if slot < 2 else 2)

    def blocks_start(flow, q):
        for slot in (0, 1):
            send_copy(flow, q, slot).start()

    def blocks_pass(flow, q):
        for slot in (0, 1):
            recv_copy(flow, q, slot).wait_recv()
            send_copy(flow, q, slot + 2).start()

    def blocks_wait(flow, q):
        for slot in (2, 3):
            recv_copy(flow, q, slot).wait_recv()

    hid_flow = (hid_piece, hb_s, hb_r)
    dgu_flow = (dgu_piece, dg_s, dg_r)

    def hidden_step(q):
        both = total(gu_flow, q)
        gate, up = both[:HC], both[HC:]
        sig = jax.nn.sigmoid(gate)
        swish = gate * sig
        hid[z, q * HC:(q + 1) * HC] = (swish * up).astype(BF16)
        blocks_start(hid_flow, q)
        c_gate[q] = up * sig * (1.0 + gate * (1.0 - sig))
        c_up[q] = swish

    def d_step(q):
        dh = total(dh_flow, q)
        dgu[z, 0, q * HC:(q + 1) * HC] = (dh * c_gate[q]).astype(BF16)
        dgu[z, 1, q * HC:(q + 1) * HC] = (dh * c_up[q]).astype(BF16)
        blocks_start(dgu_flow, q)

    def pass_copy(mine, theirs, full, send, recv, q):
        if q % 2 == 0:
            return remote(mine.at[q], theirs.at[q // 2], send.at[q], recv.at[q], other)
        return remote(mine.at[q], full.at[2 * b + q // 2], send.at[q], recv.at[q], partner)

    def down_copy(q):
        return pass_copy(g_dn, x_dn, all_dn, xd_s, xd_r, q)

    def gu_copy(q):
        return pass_copy(g_gu, x_gu, all_gu, xg_s, xg_r, q)

    def down_local(q):
        return pltpu.make_async_copy(g_dn.at[q], all_dn.at[2 * b + q // 2], loc_d.at[q // 2])

    def gu_local(q):
        return pltpu.make_async_copy(g_gu.at[q], all_gu.at[2 * b + q // 2], loc_g.at[q // 2])

    def grad_down(q):
        if q % 2:
            down_copy(q - 1).wait_recv()

        @pl.loop(0, 2)
        def _(m):
            feats = pl.ds(pl.multiple_of(m * 640, 640), 640)
            acc = None
            for t in range(4):
                part = dot_nt(hid[t, q * HC:(q + 1) * HC], xs[1, t // 2, t % 2, feats])
                acc = part if acc is None else acc + part
            if q % 2:
                acc = acc + x_dn[q // 2, :, feats].astype(F32)
            g_dn[q, :, feats] = acc.astype(BF16)

        down_copy(q).start()
        if q % 2:
            down_local(q).start()

    def grad_gate_up(q):
        if q % 2:
            gu_copy(q - 1).wait_recv()

        @pl.loop(0, 2)
        def _(m):
            feats = pl.ds(pl.multiple_of(m * 640, 640), 640)
            acc = None
            for t in range(4):
                both = jnp.concatenate(
                    [dgu[t, 0, q * HC:(q + 1) * HC], dgu[t, 1, q * HC:(q + 1) * HC]], axis=0
                )
                part = dot_nt(xs[0, t // 2, t % 2, feats], both)
                acc = part if acc is None else acc + part
            if q % 2:
                acc = acc + x_gu[q // 2, feats, :].astype(F32)
            g_gu[q, feats, :] = acc.astype(BF16)

        gu_copy(q).start()
        if q % 2:
            gu_local(q).start()

    def sum_sib(s, h):
        there = rows_of(2 * h + 1 - core)
        return remote(o_part.at[s, :, :, there], o_sib.at[s, h], sb_s.at[s, h], sb_r.at[s, h], sibling)

    def sum_terms(s, h, who, product):
        rows = rows_of(2 * h + who)

        @pl.loop(0, 4)
        def _(t):
            o_part[s, t // 2, t % 2, rows, :] = product(rows, t).astype(BF16)

    def sum_start(s, product):
        for h in range(2):
            sum_terms(s, h, 1 - core, product)
            sum_sib(s, h).start()
        for h in range(2):
            sum_terms(s, h, core, product)

    def sum_y(s, d):
        return remote(o_sum.at[s, d], o_y.at[s, d - 1], yr_s.at[s, d - 1], yr_r.at[s, d - 1], at_y(d))

    def sum_cores(s):
        for h in range(2):
            sum_sib(s, h).wait_recv()
        for d in (2, 1, 3, 0):
            yy = (y + d) % 4
            for i in range(2):
                mine = o_part[s, i, flip(yy // 2, zl), rows_of(2 * (yy % 2) + core), :].astype(F32)
                o_sum[s, d, i] = (mine + o_sib[s, yy % 2, i, flip(yy // 2, zl)].astype(F32)).astype(BF16)
            if d:
                sum_y(s, d).start()

    def sum_final(s, i):
        return remote(o_fin.at[s, i], o_got.at[s, xh], fn_s.at[s, i], fn_r.at[s, xh], spread_from(i))

    def sum_chips(s):
        for d in (1, 3, 2):
            sum_y(s, d).wait_recv()
        for i in range(2):
            total = o_sum[s, 0, i].astype(F32)
            for d in range(3):
                total = total + o_y[s, d, i].astype(F32)
            o_fin[s, i] = total.astype(BF16)

            @pl.when(jnp.logical_not(from_self(i)))
            def _(i=i):
                sum_final(s, i).start()

            @pl.when(from_self(i))
            def _(i=i):
                pltpu.make_async_copy(o_fin.at[s, i], o_got.at[s, xh], fn_r.at[s, xh]).start()

    def sum_end(s):
        for h in range(2):
            pltpu.make_async_copy(o_fin.at[s, h], o_got.at[s, h], fn_r.at[s, h]).wait()

    gate_up(0)
    gate_up(1)
    gather_pass(1)
    relay(gu_flow, 0)
    turn_other(1)
    gate_up(2)
    relay(gu_flow, 1)
    hidden_step(0)
    gather_last(1)
    gate_up(3)
    relay(gu_flow, 2)
    hidden_step(1)
    blocks_pass(hid_flow, 0)
    sib_wait_recv(1)
    weight_copy(0, 2).wait_recv()
    d_hidden(0)
    relay(gu_flow, 3)
    hidden_step(2)
    blocks_pass(hid_flow, 1)
    blocks_wait(hid_flow, 0)
    grad_down(0)
    weight_copy(1, 2).wait_recv()
    hidden_step(3)
    blocks_pass(hid_flow, 2)
    d_hidden(1)
    relay(dh_flow, 0)
    blocks_wait(hid_flow, 2)
    grad_down(2)
    blocks_pass(hid_flow, 3)
    d_hidden(2)
    relay(dh_flow, 1)
    d_step(0)
    blocks_wait(hid_flow, 1)
    grad_down(1)
    blocks_wait(hid_flow, 3)
    turn_down()
    sum_start(0, lambda rows, t: dot_nn(wdt[rows, :], hid[t]))
    d_hidden(3)
    relay(dh_flow, 2)
    d_step(1)
    blocks_pass(dgu_flow, 0)
    grad_down(3)
    sum_cores(0)
    relay(dh_flow, 3)
    d_step(2)
    blocks_pass(dgu_flow, 1)
    blocks_wait(dgu_flow, 0)
    grad_gate_up(0)
    d_step(3)
    blocks_pass(dgu_flow, 2)
    sum_chips(0)
    blocks_wait(dgu_flow, 2)
    grad_gate_up(2)
    blocks_pass(dgu_flow, 3)
    blocks_wait(dgu_flow, 1)
    blocks_wait(dgu_flow, 3)
    sum_start(1, lambda rows, t: dot_nn(wg[rows, :], dgu[t, 0]) + dot_nn(wu[rows, :], dgu[t, 1]))
    grad_gate_up(1)
    sum_cores(1)
    grad_gate_up(3)
    sum_chips(1)
    sum_end(0)
    sum_end(1)

    for q in range(NQ):
        for slot in range(6):
            term_copy(gu_flow, q, slot).wait_send()
            term_copy(dh_flow, q, slot).wait_send()
        for slot in range(4):
            send_copy(hid_flow, q, slot).wait_send()
            send_copy(dgu_flow, q, slot).wait_send()
    for s in range(2):
        spread_wait_send(s)
        for d in range(4):
            sib_copy(s, d).wait_send()
            y_copy(s, d).wait_send()
        for d in range(1, 4):
            sum_y(s, d).wait_send()
        for i in range(2):
            sum_sib(s, i).wait_send()

            @pl.when(jnp.logical_not(from_self(i)))
            def _(s=s, i=i):
                sum_final(s, i).wait_send()

    for q in range(NQ):
        down_copy(q).wait_send()
        gu_copy(q).wait_send()
        if q % 2:
            down_local(q).wait()
            gu_local(q).wait()
            down_landed = all_dn.at[2 * (1 - b) + q // 2]
            gu_landed = all_gu.at[2 * (1 - b) + q // 2]
            remote(g_dn.at[q], down_landed, xd_s.at[q], xd_r.at[q], partner).wait_recv()
            remote(g_gu.at[q], gu_landed, xg_s.at[q], xg_r.at[q], partner).wait_recv()
    for i in range(2):
        for n in range(3):
            weight_copy(i, n).wait_send()


def widen_kernel(all_gu, all_dn, got, gate, up, down, out_t, dx_t):
    gate[...] = all_gu[0, :, :HC].astype(F32)
    up[...] = all_gu[0, :, HC:].astype(F32)
    down[...] = all_dn[0].astype(F32)

    @pl.when(pl.program_id(0) == 0)
    def _():
        out_t[...] = (got[0, 0].astype(F32) + got[0, 1].astype(F32)).astype(BF16)
        dx_t[...] = (got[1, 0].astype(F32) + got[1, 1].astype(F32)).astype(BF16)


def body(x_act, grad_out, w_gate, w_up, w_down):
    hbm = pl.BlockSpec(memory_space=pl.ANY)
    dma = pltpu.SemaphoreType.DMA
    shape = jax.ShapeDtypeStruct

    def buf(*dims, dtype=BF16):
        return pltpu.VMEM(dims, dtype)

    outs = pl.pallas_call(
        layer_kernel,
        out_shape=[
            shape((2, 2, FEAT, TOK), BF16),
            shape((NQ, PANEL, 2 * HC), BF16), shape((NQ, HC, PANEL), BF16),
        ],
        in_specs=[hbm] * 5,
        out_specs=[hbm] * 3,
        scratch_shapes=[
            buf(2, 2, 2, PANEL, TOK), buf(PANEL, HID), buf(PANEL, HID), buf(HID, PANEL),
            buf(2 * HID, PANEL), buf(PANEL, HID),
            buf(NQ, 3, 2 * HC, TOK), buf(NQ, 2, HC, TOK), buf(NQ, 2, 2 * HC, TOK),
            buf(NQ, 2 * HC, TOK, dtype=F32),
            buf(NQ, 3, HC, TOK), buf(NQ, 2, HC // 2, TOK), buf(NQ, 2, HC, TOK),
            buf(NQ, HC, TOK, dtype=F32),
            buf(NQ, HC, TOK, dtype=F32), buf(NQ, HC, TOK, dtype=F32),
            buf(4, HID, TOK), buf(4, 2, HID, TOK), buf(NQ, PANEL, 2 * HC), buf(NQ, HC, PANEL),
            buf(2, PANEL, 2 * HC), buf(2, HC, PANEL),
            buf(2, 2, 2, PANEL, TOK), buf(2, 2, 2, 2, FEAT, TOK), buf(2, 4, 2, FEAT, TOK),
            buf(2, 3, 2, FEAT, TOK), buf(2, 2, FEAT, TOK),
            dma((2, 3)), dma((2, 3)), dma((2, 3)),
            dma((2, 2)), dma((2, 2)), dma((2, 4)), dma((2, 4)), dma((2, 4)), dma((2, 4)),
            dma((NQ, 6)), dma((NQ, 6)), dma((NQ, 4)), dma((NQ, 4)),
            dma((NQ, 6)), dma((NQ, 6)), dma((NQ, 4)), dma((NQ, 4)),
            dma((NQ,)), dma((NQ,)), dma((NQ,)), dma((NQ,)), dma((2,)), dma((2,)),
            dma((2, 2)), dma((2, 2)), dma((2, 3)), dma((2, 3)), dma((2, 2)), dma((2, 2)),
        ],
        name="layer",
        compiler_params=pltpu.CompilerParams(
            collective_id=0, has_side_effects=True, vmem_limit_bytes=60 * 2**20
        ),
    )(x_act[0].T, grad_out[0].T, w_gate, w_up, w_down)
    got, all_gu, all_dn = outs

    gu_block = pl.BlockSpec((1, PANEL, 2 * HC), lambda q: (q, 0, 0))
    dn_block = pl.BlockSpec((1, HC, PANEL), lambda q: (q, 0, 0))
    whole = pl.BlockSpec((FEAT, TOK), lambda q: (0, 0))
    *grads, out_t, dx_t = pl.pallas_call(
        widen_kernel,
        grid=(NQ,),
        out_shape=[
            shape((PANEL, HID), F32), shape((PANEL, HID), F32), shape((HID, PANEL), F32),
            shape((FEAT, TOK), BF16), shape((FEAT, TOK), BF16),
        ],
        in_specs=[
            gu_block, dn_block,
            pl.BlockSpec((2, 2, FEAT, TOK), lambda q: (0, 0, 0, 0)),
        ],
        out_specs=[
            pl.BlockSpec((PANEL, HC), lambda q: (0, q)),
            pl.BlockSpec((PANEL, HC), lambda q: (0, q)),
            pl.BlockSpec((HC, PANEL), lambda q: (q, 0)),
            whole, whole,
        ],
        name="widen",
        compiler_params=pltpu.CompilerParams(vmem_limit_bytes=60 * 2**20),
    )(all_gu, all_dn, got)
    return (out_t.T[None], dx_t.T[None], *grads)


def solution(mesh):
    acts = P("branch", "row", "col")
    return jax.shard_map(
        body,
        mesh=mesh,
        in_specs=(acts, acts, P("row", "col"), P("row", "col"), P("col", "row")),
        out_specs=(acts, acts, P("row", "col"), P("row", "col"), P("col", "row")),
        check_vma=False,
    )
```

```python
import functools

import jax
import jax.numpy as jnp
from jax import lax
from jax.experimental import pallas as pl
from jax.experimental.pallas import tpu as pltpu
from jax.sharding import PartitionSpec as P

MESH = pl.DeviceIdType.MESH
BF16 = jnp.bfloat16
F32 = jnp.float32

N_ROW = 4
FEAT = 320
TOK = 256
PANEL = 1280
HID = 512
NQ = 4
HC = HID // NQ


def dot_nn(left, right):
    return jnp.dot(left, right, preferred_element_type=F32)


def dot_nt(left, right):
    return lax.dot_general(left, right, (((1,), (1,)), ((), ())), preferred_element_type=F32)


def flip(a, b):
    return a + b - 2 * a * b


def layer_kernel(
    x_in, dy_in, wg_in, wu_in, wd_in,
    o_got, all_gu, all_dn,
    xs, wg, wu, wd, wgut, wdt,
    p_gu, t_gu, r_gu, o_gu, p_dh, t_dh, r_dh, o_dh, c_gate, c_up,
    hid, dgu, g_gu, g_dn, x_gu, x_dn,
    o_part, o_sib, o_sum, o_y, o_fin, o_mid,
    w_r, wf_s, wf_r,
    p0_s, p0_r, p1_s, p1_r, p2_s, p2_r,
    gu_s, gu_r, hb_s, hb_r, dh_s, dh_r, dg_s, dg_r,
    xd_s, xd_r, xg_s, xg_r, loc_d, loc_g,
    sb_s, sb_r, yr_s, yr_r, md_s, md_r, fn_s, fn_r,
):
    b, z, c = lax.axis_index("branch"), lax.axis_index("row"), lax.axis_index("col")
    y, xh, sub, core = (c // 2) % 4, c // 8, c % 4, c % 2
    yh = y // 2
    zh, zl = z // 2, z % 2
    low = flip(yh, zl)

    def at_z(d):
        return (b, (z + d) % N_ROW, c)

    def at_y(d):
        return (b, z, xh * 8 + ((y + d) % 4) * 2 + core)

    sibling = (b, z, c + 1 - 2 * core)
    partner = (1 - b, z, c)
    other = (1 - b, z, (c + 8) % 16)

    def spread_to(h):
        return (b, c // 4, h * 8 + low * 4 + sub)

    def spread_from(i):
        return (b, 2 * i + low, 4 * z + sub)

    def to_self(h):
        return (c // 4 == z) & (xh == h) & (low == yh)

    def in_plane(h):
        return (b, z, h * 8 + low * 4 + sub)

    def same_place(h):
        return (xh == h) & (low == yh)

    def same_row(i):
        return 2 * i + low == z

    def from_self(i):
        return (c // 4 == z) & (2 * i + low == z)

    def rows_of(j):
        return pl.ds(pl.multiple_of(j * FEAT, 64), FEAT)

    def remote(src, dst, ssem, rsem, to):
        return pltpu.make_async_remote_copy(
            src_ref=src, dst_ref=dst, send_sem=ssem, recv_sem=rsem, device_id=to, device_id_type=MESH
        )

    def weight_pair(i, n):
        part = pl.ds(pl.multiple_of(b * (HID // 2) + i * HC, HC), HC)
        mine, theirs = pl.ds((2 * i + 1) * HC, HC), pl.ds(2 * i * HC, HC)
        if n == 2:
            return wd_in.at[part], wd.at[mine], wd.at[theirs]
        src, dst = ((wg_in, wg), (wu_in, wu))[n]
        return src.at[:, part], dst.at[:, mine], dst.at[:, theirs]

    def weight_local(i, n):
        src, mine, _ = weight_pair(i, n)
        return pltpu.make_async_copy(src, mine, w_r.at[i, n])

    def weight_copy(i, n):
        src, _, theirs = weight_pair(i, n)
        return remote(src, theirs, wf_s.at[i, n], wf_r.at[i, n], other)

    for i in range(2):
        for n in range(3):
            weight_local(i, n).start()

    barrier = pltpu.get_barrier_semaphore()
    for to in [at_z(1), at_z(2), at_z(3), at_y(1), at_y(2), at_y(3), sibling, partner, other]:
        pl.semaphore_signal(barrier, inc=1, device_id=to, device_id_type=MESH)
    for i in range(2):
        @pl.when(jnp.logical_not(to_self(i)))
        def _(i=i):
            pl.semaphore_signal(barrier, inc=1, device_id=spread_to(i), device_id_type=MESH)

        @pl.when(jnp.logical_not(from_self(i)))
        def _(i=i):
            pl.semaphore_signal(barrier, inc=1, device_id=spread_from(i), device_id_type=MESH)

        @pl.when(jnp.logical_not(same_place(i)))
        def _(i=i):
            pl.semaphore_signal(barrier, inc=1, device_id=in_plane(i), device_id_type=MESH)

    stay = (c // 4 == z) & (low == yh)
    pl.semaphore_wait(barrier, jnp.where(stay, 11, 13) + jnp.where(low == yh, 1, 2))

    acts = (x_in, dy_in)

    def spread_copy(s, h):
        return remote(
            acts[s], xs.at[s, zh, zl, rows_of(sub)], p0_s.at[s, h], p0_r.at[s, zh], spread_to(h)
        )

    def spread_local(s):
        return pltpu.make_async_copy(
            acts[s], xs.at[s, zh, zl, rows_of(sub)], p0_r.at[s, zh]
        )

    def spread_start(s):
        for h in range(2):
            @pl.when(jnp.logical_not(to_self(h)))
            def _(h=h):
                spread_copy(s, h).start()

            @pl.when(to_self(h))
            def _():
                spread_local(s).start()

    def spread_wait_recv(s):
        for i in range(2):
            pltpu.make_async_copy(
                acts[s], xs.at[s, i, low, rows_of(sub)], p0_r.at[s, i]
            ).wait()

    def spread_wait_send(s):
        for h in range(2):
            @pl.when(jnp.logical_not(to_self(h)))
            def _(h=h):
                spread_copy(s, h).wait_send()

    def block(s, i, yy, k):
        return xs.at[s, i, flip(yy // 2, zl), rows_of(2 * (yy % 2) + k)]

    def group(s, d, k):
        yy = (y - d + 4) % 4
        return xs.at[s, :, flip(yy // 2, zl), rows_of(2 * (yy % 2) + k)]

    def y_copy(s, slot):
        if slot < 2:
            piece = group(s, 0, core)
        else:
            piece = block(s, slot - 2, (y + (3 if slot == 2 else 1)) % 4, core)
        to = at_y(1 if slot % 2 == 0 else 3)
        return remote(piece, piece, p1_s.at[s, slot], p1_r.at[s, slot], to)

    def y_wait_recv(s, slot):
        if slot < 2:
            piece = group(s, 1 if slot == 0 else 3, core)
        else:
            piece = block(s, slot - 2, (y + 2) % 4, core)
        remote(piece, piece, p1_s.at[s, slot], p1_r.at[s, slot], at_y(1)).wait_recv()

    def sib_copy(s, d):
        piece = group(s, d, core)
        return remote(piece, piece, p2_s.at[s, d], p2_r.at[s, d], sibling)

    def sib_wait_recv(s):
        for d in range(4):
            there = group(s, d, 1 - core)
            remote(there, there, p2_s.at[s, d], p2_r.at[s, d], sibling).wait_recv()

    def gather_start(s):
        y_copy(s, 0).start()
        y_copy(s, 1).start()
        sib_copy(s, 0).start()

    def gather_pass(s):
        y_wait_recv(s, 0)
        y_copy(s, 2).start()
        y_wait_recv(s, 1)
        y_copy(s, 3).start()
        sib_copy(s, 1).start()
        sib_copy(s, 3).start()

    def gather_last(s):
        y_wait_recv(s, 2)
        y_wait_recv(s, 3)
        sib_copy(s, 2).start()

    spread_start(0)

    for i, n in ((0, 0), (0, 1), (1, 0), (1, 1), (0, 2), (1, 2)):
        weight_copy(i, n).start()

    def turn(q):
        cols = pl.ds(q * HC, HC)
        wgut[q * 2 * HC:q * 2 * HC + HC, :] = wg[:, cols].T
        wgut[q * 2 * HC + HC:(q + 1) * 2 * HC, :] = wu[:, cols].T

    def turn_other(i):
        weight_copy(i, 0).wait_recv()
        weight_copy(i, 1).wait_recv()
        turn(2 * i)

    def turn_down():
        @pl.loop(0, NQ)
        def _(q):
            cols = pl.ds(pl.multiple_of(q * HC, HC), HC)
            wdt[:, cols] = wd[cols, :].T

    for i in range(2):
        for n in range(3):
            weight_local(i, n).wait()
        turn(2 * i + 1)

    spread_wait_recv(0)
    gather_start(0)
    spread_start(1)
    gather_pass(0)
    spread_wait_recv(1)
    gather_start(1)
    turn_other(0)
    gather_last(0)
    sib_wait_recv(0)

    def term_copy(flow, q, slot):
        _, parts, far, near, _, send, recv, half = flow
        rows = pl.ds((0, half, half, 0, 0, half)[slot], half)
        src = parts.at[q, (1, 1, 0, 2, 0, 2)[slot], rows]
        dst = far.at[q, slot] if slot < 2 else near.at[q, slot % 2, rows]
        return remote(src, dst, send.at[q, slot], recv.at[q, slot], at_z(3 if slot % 2 else 1))

    def terms(flow, q, lhs):
        s, parts, _, _, own, _, _, _ = flow
        for d in (2, 1, 3, 0):
            t = (z + d) % 4
            term = dot_nn(lhs, xs[s, t // 2, t % 2])
            if d == 0:
                own[q] = term
                continue
            parts[q, d - 1] = term.astype(BF16)
            for slot in {2: (0, 1), 1: (2,), 3: (3,)}[d]:
                term_copy(flow, q, slot).start()

    def relay(flow, q):
        _, parts, far, _, _, _, _, half = flow
        for slot in (0, 1):
            rows = pl.ds(slot * half, half)
            term_copy(flow, q, slot).wait_recv()
            parts[q, 2 * slot, rows, :] = (
                parts[q, 2 * slot, rows, :].astype(F32) + far[q, slot].astype(F32)
            ).astype(BF16)
            term_copy(flow, q, slot + 4).start()

    def total(flow, q):
        _, _, _, near, own, _, _, _ = flow
        for slot in (2, 3, 4, 5):
            term_copy(flow, q, slot).wait_recv()
        return own[q] + near[q, 0].astype(F32) + near[q, 1].astype(F32)

    gu_flow = (0, p_gu, t_gu, r_gu, o_gu, gu_s, gu_r, HC)
    dh_flow = (1, p_dh, t_dh, r_dh, o_dh, dh_s, dh_r, HC // 2)

    def gate_up(q):
        terms(gu_flow, q, wgut[q * 2 * HC:(q + 1) * 2 * HC, :])

    def d_hidden(q):
        terms(dh_flow, q, wd[q * HC:(q + 1) * HC, :])

    def hid_piece(q, t, half):
        if half is None:
            return hid.at[t, q * HC:(q + 1) * HC]
        return hid.at[t, q * HC + half * (HC // 2):q * HC + (half + 1) * (HC // 2)]

    def dgu_piece(q, t, half):
        rows = pl.ds(q * HC, HC)
        return dgu.at[t, :, rows] if half is None else dgu.at[t, half, rows]

    def block_copy(piece, q, slot, send, recv, step):
        part = piece(q, (z + (step, -step)[slot % 2] + 4) % 4, None if slot < 2 else slot - 2)
        return remote(part, part, send.at[q, slot], recv.at[q, slot], at_z(3 if slot % 2 else 1))

    def send_copy(flow, q, slot):
        piece, send, recv = flow
        return block_copy(piece, q, slot, send, recv, 0 if slot < 2 else 3)

    def recv_copy(flow, q, slot):
        piece, send, recv = flow
        return block_copy(piece, q, slot, send, recv, 3 if slot < 2 else 2)

    def blocks_start(flow, q):
        for slot in (0, 1):
            send_copy(flow, q, slot).start()

    def blocks_pass(flow, q):
        for slot in (0, 1):
            recv_copy(flow, q, slot).wait_recv()
            send_copy(flow, q, slot + 2).start()

    def blocks_wait(flow, q):
        for slot in (2, 3):
            recv_copy(flow, q, slot).wait_recv()

    hid_flow = (hid_piece, hb_s, hb_r)
    dgu_flow = (dgu_piece, dg_s, dg_r)

    def hidden_step(q):
        both = total(gu_flow, q)
        gate, up = both[:HC], both[HC:]
        sig = jax.nn.sigmoid(gate)
        swish = gate * sig
        hid[z, q * HC:(q + 1) * HC] = (swish * up).astype(BF16)
        blocks_start(hid_flow, q)
        c_gate[q] = up * sig * (1.0 + gate * (1.0 - sig))
        c_up[q] = swish

    def d_step(q):
        dh = total(dh_flow, q)
        dgu[z, 0, q * HC:(q + 1) * HC] = (dh * c_gate[q]).astype(BF16)
        dgu[z, 1, q * HC:(q + 1) * HC] = (dh * c_up[q]).astype(BF16)
        blocks_start(dgu_flow, q)

    def pass_copy(mine, theirs, full, send, recv, q, m, part):
        if q % 2 == 0:
            to, dst = other, theirs.at[q // 2]
        else:
            to, dst = partner, full.at[2 * b + q // 2]
        return remote(mine.at[q].at[part], dst.at[part], send.at[q, m], recv.at[q, m], to)

    def feats_of(m):
        return pl.ds(pl.multiple_of(m * (PANEL // 2), PANEL // 2), PANEL // 2)

    def down_copy(q, m):
        return pass_copy(g_dn, x_dn, all_dn, xd_s, xd_r, q, m, (slice(None), feats_of(m)))

    def gu_copy(q, m):
        return pass_copy(g_gu, x_gu, all_gu, xg_s, xg_r, q, m, (feats_of(m), slice(None)))

    def down_local(q):
        return pltpu.make_async_copy(g_dn.at[q], all_dn.at[2 * b + q // 2], loc_d.at[q // 2])

    def gu_local(q):
        return pltpu.make_async_copy(g_gu.at[q], all_gu.at[2 * b + q // 2], loc_g.at[q // 2])

    def grad_down(q):
        @pl.loop(0, 2)
        def _(m):
            feats = feats_of(m)
            acc = None
            for t in range(4):
                part = dot_nt(hid[t, q * HC:(q + 1) * HC], xs[1, t // 2, t % 2, feats])
                acc = part if acc is None else acc + part
            if q % 2:
                down_copy(q - 1, m).wait_recv()
                acc = acc + x_dn[q // 2, :, feats].astype(F32)
            g_dn[q, :, feats] = acc.astype(BF16)
            down_copy(q, m).start()

        if q % 2:
            down_local(q).start()

    def grad_gate_up(q):
        @pl.loop(0, 2)
        def _(m):
            feats = feats_of(m)
            acc = None
            for t in range(4):
                both = jnp.concatenate(
                    [dgu[t, 0, q * HC:(q + 1) * HC], dgu[t, 1, q * HC:(q + 1) * HC]], axis=0
                )
                part = dot_nt(xs[0, t // 2, t % 2, feats], both)
                acc = part if acc is None else acc + part
            if q % 2:
                gu_copy(q - 1, m).wait_recv()
                acc = acc + x_gu[q // 2, feats, :].astype(F32)
            g_gu[q, feats, :] = acc.astype(BF16)
            gu_copy(q, m).start()

        if q % 2:
            gu_local(q).start()

    def sum_sib(s, h):
        there = rows_of(2 * h + 1 - core)
        return remote(o_part.at[s, :, :, there], o_sib.at[s, h], sb_s.at[s, h], sb_r.at[s, h], sibling)

    def sum_terms(s, h, who, product):
        rows = rows_of(2 * h + who)

        @pl.loop(0, 4)
        def _(t):
            o_part[s, t // 2, t % 2, rows, :] = product(rows, t).astype(BF16)

    def sum_start(s, product):
        for h in range(2):
            sum_terms(s, h, 1 - core, product)
            sum_sib(s, h).start()
        for h in range(2):
            sum_terms(s, h, core, product)

    def sum_y(s, d):
        return remote(o_sum.at[s, d], o_y.at[s, d - 1], yr_s.at[s, d - 1], yr_r.at[s, d - 1], at_y(d))

    def sum_cores(s):
        for h in range(2):
            sum_sib(s, h).wait_recv()
        for d in (2, 1, 3, 0):
            yy = (y + d) % 4
            for i in range(2):
                mine = o_part[s, i, flip(yy // 2, zl), rows_of(2 * (yy % 2) + core), :].astype(F32)
                o_sum[s, d, i] = (mine + o_sib[s, yy % 2, i, flip(yy // 2, zl)].astype(F32)).astype(BF16)
            if d:
                sum_y(s, d).start()

    def sum_mid(s, i):
        to = (b, 2 * i + low, c)
        return remote(o_fin.at[s, i], o_mid.at[s, zh], md_s.at[s, i], md_r.at[s, zh], to)

    def sum_final(s, h):
        return remote(o_mid.at[s, h], o_got.at[s, xh], fn_s.at[s, h], fn_r.at[s, xh], in_plane(h))

    def sum_turn(s):
        for h in range(2):
            pltpu.make_async_copy(o_fin.at[s, h], o_mid.at[s, h], md_r.at[s, h]).wait()

            @pl.when(jnp.logical_not(same_place(h)))
            def _(h=h):
                sum_final(s, h).start()

            @pl.when(same_place(h))
            def _(h=h):
                pltpu.make_async_copy(o_mid.at[s, h], o_got.at[s, xh], fn_r.at[s, xh]).start()

    def sum_chips(s):
        for d in (1, 3, 2):
            sum_y(s, d).wait_recv()
        for i in range(2):
            total = o_sum[s, 0, i].astype(F32)
            for d in range(3):
                total = total + o_y[s, d, i].astype(F32)
            o_fin[s, i] = total.astype(BF16)

            @pl.when(jnp.logical_not(same_row(i)))
            def _(i=i):
                sum_mid(s, i).start()

            @pl.when(same_row(i))
            def _(i=i):
                pltpu.make_async_copy(o_fin.at[s, i], o_mid.at[s, zh], md_r.at[s, zh]).start()

    def sum_end(s):
        for h in range(2):
            pltpu.make_async_copy(o_mid.at[s, h], o_got.at[s, h], fn_r.at[s, h]).wait()

    gate_up(0)
    gate_up(1)
    gather_pass(1)
    relay(gu_flow, 0)
    gate_up(3)
    relay(gu_flow, 1)
    hidden_step(0)
    gather_last(1)
    turn_other(1)
    gate_up(2)
    relay(gu_flow, 3)
    hidden_step(1)
    blocks_pass(hid_flow, 0)
    sib_wait_recv(1)
    d_hidden(1)
    relay(gu_flow, 2)
    hidden_step(3)
    blocks_pass(hid_flow, 1)
    blocks_wait(hid_flow, 0)
    grad_down(0)
    weight_copy(0, 2).wait_recv()
    d_hidden(0)
    relay(dh_flow, 1)
    hidden_step(2)
    blocks_pass(hid_flow, 3)
    blocks_wait(hid_flow, 1)
    blocks_pass(hid_flow, 2)
    weight_copy(1, 2).wait_recv()
    d_hidden(2)
    relay(dh_flow, 0)
    d_step(1)
    blocks_wait(hid_flow, 2)
    grad_down(2)
    blocks_wait(hid_flow, 3)
    turn_down()
    sum_start(0, lambda rows, t: dot_nn(wdt[rows, :], hid[t]))
    d_hidden(3)
    relay(dh_flow, 2)
    d_step(0)
    blocks_pass(dgu_flow, 1)
    grad_down(1)
    sum_cores(0)
    relay(dh_flow, 3)
    d_step(2)
    blocks_pass(dgu_flow, 0)
    blocks_wait(dgu_flow, 1)
    d_step(3)
    blocks_pass(dgu_flow, 2)
    blocks_wait(dgu_flow, 0)
    grad_gate_up(0)
    blocks_pass(dgu_flow, 3)
    blocks_wait(dgu_flow, 2)
    grad_gate_up(2)
    grad_down(3)
    blocks_wait(dgu_flow, 3)
    sum_start(1, lambda rows, t: dot_nn(wg[rows, :], dgu[t, 0]) + dot_nn(wu[rows, :], dgu[t, 1]))
    sum_cores(1)
    sum_chips(0)
    grad_gate_up(1)
    sum_turn(0)
    sum_chips(1)
    grad_gate_up(3)
    sum_turn(1)
    sum_end(0)
    sum_end(1)

    for q in range(NQ):
        for slot in range(6):
            term_copy(gu_flow, q, slot).wait_send()
            term_copy(dh_flow, q, slot).wait_send()
        for slot in range(4):
            send_copy(hid_flow, q, slot).wait_send()
            send_copy(dgu_flow, q, slot).wait_send()
    for s in range(2):
        spread_wait_send(s)
        for d in range(4):
            sib_copy(s, d).wait_send()
            y_copy(s, d).wait_send()
        for d in range(1, 4):
            sum_y(s, d).wait_send()
        for i in range(2):
            sum_sib(s, i).wait_send()

            @pl.when(jnp.logical_not(same_row(i)))
            def _(s=s, i=i):
                sum_mid(s, i).wait_send()

            @pl.when(jnp.logical_not(same_place(i)))
            def _(s=s, i=i):
                sum_final(s, i).wait_send()

    for q in range(NQ):
        for m in range(2):
            down_copy(q, m).wait_send()
            gu_copy(q, m).wait_send()
        if q % 2:
            down_local(q).wait()
            gu_local(q).wait()
            slot = 2 * (1 - b) + q // 2
            for m in range(2):
                down_landed = all_dn.at[slot, :, feats_of(m)]
                gu_landed = all_gu.at[slot, feats_of(m), :]
                remote(down_landed, down_landed, xd_s.at[q, m], xd_r.at[q, m], partner).wait_recv()
                remote(gu_landed, gu_landed, xg_s.at[q, m], xg_r.at[q, m], partner).wait_recv()
    for i in range(2):
        for n in range(3):
            weight_copy(i, n).wait_send()


def widen_kernel(all_gu, all_dn, got, gate, up, down, out_t, dx_t):
    gate[...] = all_gu[0, :, :HC].astype(F32)
    up[...] = all_gu[0, :, HC:].astype(F32)
    down[...] = all_dn[0].astype(F32)

    @pl.when(pl.program_id(0) == 0)
    def _():
        out_t[...] = (got[0, 0].astype(F32) + got[0, 1].astype(F32)).astype(BF16)
        dx_t[...] = (got[1, 0].astype(F32) + got[1, 1].astype(F32)).astype(BF16)


def body(x_act, grad_out, w_gate, w_up, w_down):
    hbm = pl.BlockSpec(memory_space=pl.ANY)
    dma = pltpu.SemaphoreType.DMA
    shape = jax.ShapeDtypeStruct

    def buf(*dims, dtype=BF16):
        return pltpu.VMEM(dims, dtype)

    outs = pl.pallas_call(
        layer_kernel,
        out_shape=[
            shape((2, 2, FEAT, TOK), BF16),
            shape((NQ, PANEL, 2 * HC), BF16), shape((NQ, HC, PANEL), BF16),
        ],
        in_specs=[hbm] * 5,
        out_specs=[hbm] * 3,
        scratch_shapes=[
            buf(2, 2, 2, PANEL, TOK), buf(PANEL, HID), buf(PANEL, HID), buf(HID, PANEL),
            buf(2 * HID, PANEL), buf(PANEL, HID),
            buf(NQ, 3, 2 * HC, TOK), buf(NQ, 2, HC, TOK), buf(NQ, 2, 2 * HC, TOK),
            buf(NQ, 2 * HC, TOK, dtype=F32),
            buf(NQ, 3, HC, TOK), buf(NQ, 2, HC // 2, TOK), buf(NQ, 2, HC, TOK),
            buf(NQ, HC, TOK, dtype=F32),
            buf(NQ, HC, TOK, dtype=F32), buf(NQ, HC, TOK, dtype=F32),
            buf(4, HID, TOK), buf(4, 2, HID, TOK), buf(NQ, PANEL, 2 * HC), buf(NQ, HC, PANEL),
            buf(2, PANEL, 2 * HC), buf(2, HC, PANEL),
            buf(2, 2, 2, PANEL, TOK), buf(2, 2, 2, 2, FEAT, TOK), buf(2, 4, 2, FEAT, TOK),
            buf(2, 3, 2, FEAT, TOK), buf(2, 2, FEAT, TOK), buf(2, 2, FEAT, TOK),
            dma((2, 3)), dma((2, 3)), dma((2, 3)),
            dma((2, 2)), dma((2, 2)), dma((2, 4)), dma((2, 4)), dma((2, 4)), dma((2, 4)),
            dma((NQ, 6)), dma((NQ, 6)), dma((NQ, 4)), dma((NQ, 4)),
            dma((NQ, 6)), dma((NQ, 6)), dma((NQ, 4)), dma((NQ, 4)),
            dma((NQ, 2)), dma((NQ, 2)), dma((NQ, 2)), dma((NQ, 2)), dma((2,)), dma((2,)),
            dma((2, 2)), dma((2, 2)), dma((2, 3)), dma((2, 3)),
            dma((2, 2)), dma((2, 2)), dma((2, 2)), dma((2, 2)),
        ],
        name="layer",
        compiler_params=pltpu.CompilerParams(
            collective_id=0, has_side_effects=True, vmem_limit_bytes=60 * 2**20
        ),
    )(x_act[0].T, grad_out[0].T, w_gate, w_up, w_down)
    got, all_gu, all_dn = outs

    gu_block = pl.BlockSpec((1, PANEL, 2 * HC), lambda q: (q, 0, 0))
    dn_block = pl.BlockSpec((1, HC, PANEL), lambda q: (q, 0, 0))
    whole = pl.BlockSpec((FEAT, TOK), lambda q: (0, 0))
    *grads, out_t, dx_t = pl.pallas_call(
        widen_kernel,
        grid=(NQ,),
        out_shape=[
            shape((PANEL, HID), F32), shape((PANEL, HID), F32), shape((HID, PANEL), F32),
            shape((FEAT, TOK), BF16), shape((FEAT, TOK), BF16),
        ],
        in_specs=[
            gu_block, dn_block,
            pl.BlockSpec((2, 2, FEAT, TOK), lambda q: (0, 0, 0, 0)),
        ],
        out_specs=[
            pl.BlockSpec((PANEL, HC), lambda q: (0, q)),
            pl.BlockSpec((PANEL, HC), lambda q: (0, q)),
            pl.BlockSpec((HC, PANEL), lambda q: (q, 0)),
            whole, whole,
        ],
        name="widen",
        compiler_params=pltpu.CompilerParams(vmem_limit_bytes=60 * 2**20),
    )(all_gu, all_dn, got)
    return (out_t.T[None], dx_t.T[None], *grads)


def solution(mesh):
    acts = P("branch", "row", "col")
    return jax.shard_map(
        body,
        mesh=mesh,
        in_specs=(acts, acts, P("row", "col"), P("row", "col"), P("col", "row")),
        out_specs=(acts, acts, P("row", "col"), P("row", "col"), P("col", "row")),
        check_vma=False,
    )
```

```python
import functools

import jax
import jax.numpy as jnp
from jax import lax
from jax.experimental import pallas as pl
from jax.experimental.pallas import tpu as pltpu
from jax.sharding import PartitionSpec as P

MESH = pl.DeviceIdType.MESH
BF16 = jnp.bfloat16
F32 = jnp.float32

N_ROW = 4
FEAT = 320
TOK = 256
PANEL = 1280
HID = 512
NQ = 4
HC = HID // NQ


def dot_nn(left, right):
    return jnp.dot(left, right, preferred_element_type=F32)


def dot_nt(left, right):
    return lax.dot_general(left, right, (((1,), (1,)), ((), ())), preferred_element_type=F32)


def flip(a, b):
    return a + b - 2 * a * b


def layer_kernel(
    x_in, dy_in, wg_in, wu_in, wd_in,
    o_got, all_gu, all_dn,
    xs, wg, wu, wd, wgut, wdt,
    p_gu, t_gu, r_gu, o_gu, p_dh, t_dh, r_dh, o_dh, c_gate, c_up,
    hid, dgu, g_gu, g_dn, x_gu, x_dn,
    o_part, o_sib, o_sum, o_far, o_y, o_fin, o_mid,
    w_r, wf_s, wf_r,
    p0_s, p0_r, p1_s, p1_r, p2_s, p2_r,
    gu_s, gu_r, hb_s, hb_r, dh_s, dh_r, dg_s, dg_r,
    xd_s, xd_r, xg_s, xg_r, loc_d, loc_g,
    sb_s, sb_r, yr_s, yr_r, md_s, md_r, fn_s, fn_r,
):
    b, z, c = lax.axis_index("branch"), lax.axis_index("row"), lax.axis_index("col")
    y, xh, sub, core = (c // 2) % 4, c // 8, c % 4, c % 2
    yh = y // 2
    zh, zl = z // 2, z % 2
    low = flip(yh, zl)

    def at_z(d):
        return (b, (z + d) % N_ROW, c)

    def at_y(d):
        return (b, z, xh * 8 + ((y + d) % 4) * 2 + core)

    sibling = (b, z, c + 1 - 2 * core)
    partner = (1 - b, z, c)
    other = (1 - b, z, (c + 8) % 16)

    def spread_to(h):
        return (b, c // 4, h * 8 + low * 4 + sub)

    def spread_from(i):
        return (b, 2 * i + low, 4 * z + sub)

    def to_self(h):
        return (c // 4 == z) & (xh == h) & (low == yh)

    def in_plane(h):
        return (b, z, h * 8 + low * 4 + sub)

    def same_place(h):
        return (xh == h) & (low == yh)

    def same_row(i):
        return 2 * i + low == z

    def from_self(i):
        return (c // 4 == z) & (2 * i + low == z)

    def rows_of(j):
        return pl.ds(pl.multiple_of(j * FEAT, 64), FEAT)

    def remote(src, dst, ssem, rsem, to):
        return pltpu.make_async_remote_copy(
            src_ref=src, dst_ref=dst, send_sem=ssem, recv_sem=rsem, device_id=to, device_id_type=MESH
        )

    def weight_pair(i, n):
        part = pl.ds(pl.multiple_of(b * (HID // 2) + i * HC, HC), HC)
        mine, theirs = pl.ds((2 * i + 1) * HC, HC), pl.ds(2 * i * HC, HC)
        if n == 2:
            return wd_in.at[part], wd.at[mine], wd.at[theirs]
        src, dst = ((wg_in, wg), (wu_in, wu))[n]
        return src.at[:, part], dst.at[:, mine], dst.at[:, theirs]

    def weight_local(i, n):
        src, mine, _ = weight_pair(i, n)
        return pltpu.make_async_copy(src, mine, w_r.at[i, n])

    def weight_copy(i, n):
        src, _, theirs = weight_pair(i, n)
        return remote(src, theirs, wf_s.at[i, n], wf_r.at[i, n], other)

    for i in range(2):
        for n in range(3):
            weight_local(i, n).start()

    barrier = pltpu.get_barrier_semaphore()
    for to in [at_z(1), at_z(2), at_z(3), at_y(1), at_y(2), at_y(3), sibling, partner, other]:
        pl.semaphore_signal(barrier, inc=1, device_id=to, device_id_type=MESH)
    for i in range(2):
        @pl.when(jnp.logical_not(to_self(i)))
        def _(i=i):
            pl.semaphore_signal(barrier, inc=1, device_id=spread_to(i), device_id_type=MESH)

        @pl.when(jnp.logical_not(from_self(i)))
        def _(i=i):
            pl.semaphore_signal(barrier, inc=1, device_id=spread_from(i), device_id_type=MESH)

        @pl.when(jnp.logical_not(same_place(i)))
        def _(i=i):
            pl.semaphore_signal(barrier, inc=1, device_id=in_plane(i), device_id_type=MESH)

    stay = (c // 4 == z) & (low == yh)
    pl.semaphore_wait(barrier, jnp.where(stay, 11, 13) + jnp.where(low == yh, 1, 2))

    acts = (x_in, dy_in)

    def spread_copy(s, h):
        return remote(
            acts[s], xs.at[s, zh, zl, rows_of(sub)], p0_s.at[s, h], p0_r.at[s, zh], spread_to(h)
        )

    def spread_local(s):
        return pltpu.make_async_copy(
            acts[s], xs.at[s, zh, zl, rows_of(sub)], p0_r.at[s, zh]
        )

    def spread_start(s):
        for h in range(2):
            @pl.when(jnp.logical_not(to_self(h)))
            def _(h=h):
                spread_copy(s, h).start()

            @pl.when(to_self(h))
            def _():
                spread_local(s).start()

    def spread_wait_recv(s):
        for i in range(2):
            pltpu.make_async_copy(
                acts[s], xs.at[s, i, low, rows_of(sub)], p0_r.at[s, i]
            ).wait()

    def spread_wait_send(s):
        for h in range(2):
            @pl.when(jnp.logical_not(to_self(h)))
            def _(h=h):
                spread_copy(s, h).wait_send()

    def block(s, i, yy, k):
        return xs.at[s, i, flip(yy // 2, zl), rows_of(2 * (yy % 2) + k)]

    def group(s, d, k):
        yy = (y - d + 4) % 4
        return xs.at[s, :, flip(yy // 2, zl), rows_of(2 * (yy % 2) + k)]

    def y_copy(s, slot):
        if slot < 2:
            piece = group(s, 0, core)
        else:
            piece = block(s, slot - 2, (y + (3 if slot == 2 else 1)) % 4, core)
        to = at_y(1 if slot % 2 == 0 else 3)
        return remote(piece, piece, p1_s.at[s, slot], p1_r.at[s, slot], to)

    def y_wait_recv(s, slot):
        if slot < 2:
            piece = group(s, 1 if slot == 0 else 3, core)
        else:
            piece = block(s, slot - 2, (y + 2) % 4, core)
        remote(piece, piece, p1_s.at[s, slot], p1_r.at[s, slot], at_y(1)).wait_recv()

    def sib_copy(s, d):
        piece = group(s, d, core)
        return remote(piece, piece, p2_s.at[s, d], p2_r.at[s, d], sibling)

    def sib_wait_recv(s):
        for d in range(4):
            there = group(s, d, 1 - core)
            remote(there, there, p2_s.at[s, d], p2_r.at[s, d], sibling).wait_recv()

    def gather_start(s):
        y_copy(s, 0).start()
        y_copy(s, 1).start()
        sib_copy(s, 0).start()

    def gather_pass(s):
        y_wait_recv(s, 0)
        y_copy(s, 2).start()
        y_wait_recv(s, 1)
        y_copy(s, 3).start()
        sib_copy(s, 1).start()
        sib_copy(s, 3).start()

    def gather_last(s):
        y_wait_recv(s, 2)
        y_wait_recv(s, 3)
        sib_copy(s, 2).start()

    spread_start(0)

    for i, n in ((0, 0), (0, 1), (1, 0), (1, 1), (0, 2), (1, 2)):
        weight_copy(i, n).start()

    def turn(q):
        cols = pl.ds(q * HC, HC)
        wgut[q * 2 * HC:q * 2 * HC + HC, :] = wg[:, cols].T
        wgut[q * 2 * HC + HC:(q + 1) * 2 * HC, :] = wu[:, cols].T

    def turn_other(i):
        weight_copy(i, 0).wait_recv()
        weight_copy(i, 1).wait_recv()
        turn(2 * i)

    def turn_down():
        @pl.loop(0, NQ)
        def _(q):
            cols = pl.ds(pl.multiple_of(q * HC, HC), HC)
            wdt[:, cols] = wd[cols, :].T

    for i in range(2):
        for n in range(3):
            weight_local(i, n).wait()
        turn(2 * i + 1)

    spread_wait_recv(0)
    gather_start(0)
    spread_start(1)
    gather_pass(0)
    spread_wait_recv(1)
    gather_start(1)
    turn_other(0)
    gather_last(0)
    sib_wait_recv(0)

    def term_copy(flow, q, slot):
        _, parts, far, near, _, send, recv, half = flow
        rows = pl.ds((0, half, half, 0, 0, half)[slot], half)
        src = parts.at[q, (1, 1, 0, 2, 0, 2)[slot], rows]
        dst = far.at[q, slot] if slot < 2 else near.at[q, slot % 2, rows]
        return remote(src, dst, send.at[q, slot], recv.at[q, slot], at_z(3 if slot % 2 else 1))

    def terms(flow, q, lhs):
        s, parts, _, _, own, _, _, _ = flow
        for d in (2, 1, 3, 0):
            t = (z + d) % 4
            term = dot_nn(lhs, xs[s, t // 2, t % 2])
            if d == 0:
                own[q] = term
                continue
            parts[q, d - 1] = term.astype(BF16)
            for slot in {2: (0, 1), 1: (2,), 3: (3,)}[d]:
                term_copy(flow, q, slot).start()

    def relay(flow, q):
        _, parts, far, _, _, _, _, half = flow
        for slot in (0, 1):
            rows = pl.ds(slot * half, half)
            term_copy(flow, q, slot).wait_recv()
            parts[q, 2 * slot, rows, :] = (
                parts[q, 2 * slot, rows, :].astype(F32) + far[q, slot].astype(F32)
            ).astype(BF16)
            term_copy(flow, q, slot + 4).start()

    def total(flow, q):
        _, _, _, near, own, _, _, _ = flow
        for slot in (2, 3, 4, 5):
            term_copy(flow, q, slot).wait_recv()
        return own[q] + near[q, 0].astype(F32) + near[q, 1].astype(F32)

    gu_flow = (0, p_gu, t_gu, r_gu, o_gu, gu_s, gu_r, HC)
    dh_flow = (1, p_dh, t_dh, r_dh, o_dh, dh_s, dh_r, HC // 2)

    def gate_up(q):
        terms(gu_flow, q, wgut[q * 2 * HC:(q + 1) * 2 * HC, :])

    def d_hidden(q):
        terms(dh_flow, q, wd[q * HC:(q + 1) * HC, :])

    def hid_piece(q, t, half):
        if half is None:
            return hid.at[t, q * HC:(q + 1) * HC]
        return hid.at[t, q * HC + half * (HC // 2):q * HC + (half + 1) * (HC // 2)]

    def dgu_piece(q, t, half):
        rows = pl.ds(q * HC, HC)
        return dgu.at[t, :, rows] if half is None else dgu.at[t, half, rows]

    def block_copy(piece, q, slot, send, recv, step):
        part = piece(q, (z + (step, -step)[slot % 2] + 4) % 4, None if slot < 2 else slot - 2)
        return remote(part, part, send.at[q, slot], recv.at[q, slot], at_z(3 if slot % 2 else 1))

    def send_copy(flow, q, slot):
        piece, send, recv = flow
        return block_copy(piece, q, slot, send, recv, 0 if slot < 2 else 3)

    def recv_copy(flow, q, slot):
        piece, send, recv = flow
        return block_copy(piece, q, slot, send, recv, 3 if slot < 2 else 2)

    def blocks_start(flow, q):
        for slot in (0, 1):
            send_copy(flow, q, slot).start()

    def blocks_pass(flow, q):
        for slot in (0, 1):
            recv_copy(flow, q, slot).wait_recv()
            send_copy(flow, q, slot + 2).start()

    def blocks_wait(flow, q):
        for slot in (2, 3):
            recv_copy(flow, q, slot).wait_recv()

    hid_flow = (hid_piece, hb_s, hb_r)
    dgu_flow = (dgu_piece, dg_s, dg_r)

    def hidden_step(q):
        both = total(gu_flow, q)
        gate, up = both[:HC], both[HC:]
        sig = jax.nn.sigmoid(gate)
        swish = gate * sig
        hid[z, q * HC:(q + 1) * HC] = (swish * up).astype(BF16)
        blocks_start(hid_flow, q)
        c_gate[q] = up * sig * (1.0 + gate * (1.0 - sig))
        c_up[q] = swish

    def d_step(q):
        dh = total(dh_flow, q)
        dgu[z, 0, q * HC:(q + 1) * HC] = (dh * c_gate[q]).astype(BF16)
        dgu[z, 1, q * HC:(q + 1) * HC] = (dh * c_up[q]).astype(BF16)
        blocks_start(dgu_flow, q)

    def pass_copy(mine, theirs, full, send, recv, q, m, part):
        if q % 2 == 0:
            to, dst = other, theirs.at[q // 2]
        else:
            to, dst = partner, full.at[2 * b + q // 2]
        return remote(mine.at[q].at[part], dst.at[part], send.at[q, m], recv.at[q, m], to)

    def feats_of(m):
        return pl.ds(pl.multiple_of(m * (PANEL // 2), PANEL // 2), PANEL // 2)

    def down_copy(q, m):
        return pass_copy(g_dn, x_dn, all_dn, xd_s, xd_r, q, m, (slice(None), feats_of(m)))

    def gu_copy(q, m):
        return pass_copy(g_gu, x_gu, all_gu, xg_s, xg_r, q, m, (feats_of(m), slice(None)))

    def down_local(q):
        return pltpu.make_async_copy(g_dn.at[q], all_dn.at[2 * b + q // 2], loc_d.at[q // 2])

    def gu_local(q):
        return pltpu.make_async_copy(g_gu.at[q], all_gu.at[2 * b + q // 2], loc_g.at[q // 2])

    def grad_down(q):
        @pl.loop(0, 2)
        def _(m):
            feats = feats_of(m)
            acc = None
            for t in range(4):
                part = dot_nt(hid[t, q * HC:(q + 1) * HC], xs[1, t // 2, t % 2, feats])
                acc = part if acc is None else acc + part
            if q % 2:
                down_copy(q - 1, m).wait_recv()
                acc = acc + x_dn[q // 2, :, feats].astype(F32)
            g_dn[q, :, feats] = acc.astype(BF16)
            down_copy(q, m).start()

        if q % 2:
            down_local(q).start()

    def grad_gate_up(q):
        @pl.loop(0, 2)
        def _(m):
            feats = feats_of(m)
            acc = None
            for t in range(4):
                both = jnp.concatenate(
                    [dgu[t, 0, q * HC:(q + 1) * HC], dgu[t, 1, q * HC:(q + 1) * HC]], axis=0
                )
                part = dot_nt(xs[0, t // 2, t % 2, feats], both)
                acc = part if acc is None else acc + part
            if q % 2:
                gu_copy(q - 1, m).wait_recv()
                acc = acc + x_gu[q // 2, feats, :].astype(F32)
            g_gu[q, feats, :] = acc.astype(BF16)
            gu_copy(q, m).start()

        if q % 2:
            gu_local(q).start()

    def sum_sib(s, h):
        there = rows_of(2 * h + 1 - core)
        return remote(o_part.at[s, :, :, there], o_sib.at[s, h], sb_s.at[s, h], sb_r.at[s, h], sibling)

    def sum_terms(s, h, who, product):
        rows = rows_of(2 * h + who)

        @pl.loop(0, 4)
        def _(t):
            o_part[s, t // 2, t % 2, rows, :] = product(rows, t).astype(BF16)

    def sum_start(s, product):
        for h in range(2):
            sum_terms(s, h, 1 - core, product)
            sum_sib(s, h).start()
        for h in range(2):
            sum_terms(s, h, core, product)

    def sum_y(s, slot):
        i = (0, 1, 1, 0, 0, 1)[slot]
        src = o_sum.at[s, (2, 2, 1, 3, 1, 3)[slot], i]
        dst = o_far.at[s, slot] if slot < 2 else o_y.at[s, slot % 2, i]
        return remote(src, dst, yr_s.at[s, slot], yr_r.at[s, slot], at_y(3 if slot % 2 else 1))

    def sum_relay(s):
        for slot in (0, 1):
            sum_y(s, slot).wait_recv()
            d = 1 + 2 * slot
            o_sum[s, d, slot] = (o_sum[s, d, slot].astype(F32) + o_far[s, slot].astype(F32)).astype(BF16)
            sum_y(s, slot + 4).start()

    def sum_cores(s):
        for h in range(2):
            sum_sib(s, h).wait_recv()
        for d in (2, 1, 3, 0):
            yy = (y + d) % 4
            for i in range(2):
                mine = o_part[s, i, flip(yy // 2, zl), rows_of(2 * (yy % 2) + core), :].astype(F32)
                o_sum[s, d, i] = (mine + o_sib[s, yy % 2, i, flip(yy // 2, zl)].astype(F32)).astype(BF16)
            for slot in ((), (2,), (0, 1), (3,))[d]:
                sum_y(s, slot).start()

    def sum_mid(s, i):
        to = (b, 2 * i + low, c)
        return remote(o_fin.at[s, i], o_mid.at[s, zh], md_s.at[s, i], md_r.at[s, zh], to)

    def sum_final(s, h):
        return remote(o_mid.at[s, h], o_got.at[s, xh], fn_s.at[s, h], fn_r.at[s, xh], in_plane(h))

    def sum_turn(s):
        for h in range(2):
            pltpu.make_async_copy(o_fin.at[s, h], o_mid.at[s, h], md_r.at[s, h]).wait()

            @pl.when(jnp.logical_not(same_place(h)))
            def _(h=h):
                sum_final(s, h).start()

            @pl.when(same_place(h))
            def _(h=h):
                pltpu.make_async_copy(o_mid.at[s, h], o_got.at[s, xh], fn_r.at[s, xh]).start()

    def sum_chips(s):
        for slot in (2, 3, 4, 5):
            sum_y(s, slot).wait_recv()
        for i in range(2):
            total = o_sum[s, 0, i].astype(F32)
            for d in range(2):
                total = total + o_y[s, d, i].astype(F32)
            o_fin[s, i] = total.astype(BF16)

            @pl.when(jnp.logical_not(same_row(i)))
            def _(i=i):
                sum_mid(s, i).start()

            @pl.when(same_row(i))
            def _(i=i):
                pltpu.make_async_copy(o_fin.at[s, i], o_mid.at[s, zh], md_r.at[s, zh]).start()

    def sum_end(s):
        for h in range(2):
            pltpu.make_async_copy(o_mid.at[s, h], o_got.at[s, h], fn_r.at[s, h]).wait()

    gate_up(0)
    gate_up(1)
    gather_pass(1)
    relay(gu_flow, 0)
    gate_up(3)
    relay(gu_flow, 1)
    hidden_step(0)
    gather_last(1)
    turn_other(1)
    gate_up(2)
    relay(gu_flow, 3)
    hidden_step(1)
    blocks_pass(hid_flow, 0)
    sib_wait_recv(1)
    d_hidden(1)
    relay(gu_flow, 2)
    hidden_step(3)
    blocks_pass(hid_flow, 1)
    blocks_wait(hid_flow, 0)
    grad_down(0)
    weight_copy(0, 2).wait_recv()
    d_hidden(0)
    relay(dh_flow, 1)
    hidden_step(2)
    blocks_pass(hid_flow, 3)
    blocks_wait(hid_flow, 1)
    blocks_pass(hid_flow, 2)
    weight_copy(1, 2).wait_recv()
    d_hidden(2)
    relay(dh_flow, 0)
    d_step(1)
    blocks_wait(hid_flow, 2)
    grad_down(2)
    blocks_wait(hid_flow, 3)
    turn_down()
    sum_start(0, lambda rows, t: dot_nn(wdt[rows, :], hid[t]))
    d_hidden(3)
    relay(dh_flow, 2)
    d_step(0)
    blocks_pass(dgu_flow, 1)
    grad_down(1)
    sum_cores(0)
    relay(dh_flow, 3)
    d_step(2)
    blocks_pass(dgu_flow, 0)
    blocks_wait(dgu_flow, 1)
    sum_relay(0)
    d_step(3)
    blocks_pass(dgu_flow, 2)
    blocks_wait(dgu_flow, 0)
    grad_gate_up(0)
    blocks_pass(dgu_flow, 3)
    blocks_wait(dgu_flow, 2)
    grad_gate_up(2)
    grad_down(3)
    blocks_wait(dgu_flow, 3)
    sum_start(1, lambda rows, t: dot_nn(wg[rows, :], dgu[t, 0]) + dot_nn(wu[rows, :], dgu[t, 1]))
    grad_gate_up(1)
    sum_cores(1)
    sum_chips(0)
    sum_relay(1)
    sum_turn(0)
    sum_chips(1)
    grad_gate_up(3)
    sum_turn(1)
    sum_end(0)
    sum_end(1)

    for q in range(NQ):
        for slot in range(6):
            term_copy(gu_flow, q, slot).wait_send()
            term_copy(dh_flow, q, slot).wait_send()
        for slot in range(4):
            send_copy(hid_flow, q, slot).wait_send()
            send_copy(dgu_flow, q, slot).wait_send()
    for s in range(2):
        spread_wait_send(s)
        for d in range(4):
            sib_copy(s, d).wait_send()
            y_copy(s, d).wait_send()
        for slot in range(6):
            sum_y(s, slot).wait_send()
        for i in range(2):
            sum_sib(s, i).wait_send()

            @pl.when(jnp.logical_not(same_row(i)))
            def _(s=s, i=i):
                sum_mid(s, i).wait_send()

            @pl.when(jnp.logical_not(same_place(i)))
            def _(s=s, i=i):
                sum_final(s, i).wait_send()

    for q in range(NQ):
        for m in range(2):
            down_copy(q, m).wait_send()
            gu_copy(q, m).wait_send()
        if q % 2:
            down_local(q).wait()
            gu_local(q).wait()
            slot = 2 * (1 - b) + q // 2
            for m in range(2):
                down_landed = all_dn.at[slot, :, feats_of(m)]
                gu_landed = all_gu.at[slot, feats_of(m), :]
                remote(down_landed, down_landed, xd_s.at[q, m], xd_r.at[q, m], partner).wait_recv()
                remote(gu_landed, gu_landed, xg_s.at[q, m], xg_r.at[q, m], partner).wait_recv()
    for i in range(2):
        for n in range(3):
            weight_copy(i, n).wait_send()


def widen_kernel(all_gu, all_dn, got, gate, up, down, out_t, dx_t):
    gate[...] = all_gu[0, :, :HC].astype(F32)
    up[...] = all_gu[0, :, HC:].astype(F32)
    down[...] = all_dn[0].astype(F32)

    @pl.when(pl.program_id(0) == 0)
    def _():
        out_t[...] = (got[0, 0].astype(F32) + got[0, 1].astype(F32)).astype(BF16)
        dx_t[...] = (got[1, 0].astype(F32) + got[1, 1].astype(F32)).astype(BF16)


def body(x_act, grad_out, w_gate, w_up, w_down):
    hbm = pl.BlockSpec(memory_space=pl.ANY)
    dma = pltpu.SemaphoreType.DMA
    shape = jax.ShapeDtypeStruct

    def buf(*dims, dtype=BF16):
        return pltpu.VMEM(dims, dtype)

    outs = pl.pallas_call(
        layer_kernel,
        out_shape=[
            shape((2, 2, FEAT, TOK), BF16),
            shape((NQ, PANEL, 2 * HC), BF16), shape((NQ, HC, PANEL), BF16),
        ],
        in_specs=[hbm] * 5,
        out_specs=[hbm] * 3,
        scratch_shapes=[
            buf(2, 2, 2, PANEL, TOK), buf(PANEL, HID), buf(PANEL, HID), buf(HID, PANEL),
            buf(2 * HID, PANEL), buf(PANEL, HID),
            buf(NQ, 3, 2 * HC, TOK), buf(NQ, 2, HC, TOK), buf(NQ, 2, 2 * HC, TOK),
            buf(NQ, 2 * HC, TOK, dtype=F32),
            buf(NQ, 3, HC, TOK), buf(NQ, 2, HC // 2, TOK), buf(NQ, 2, HC, TOK),
            buf(NQ, HC, TOK, dtype=F32),
            buf(NQ, HC, TOK, dtype=F32), buf(NQ, HC, TOK, dtype=F32),
            buf(4, HID, TOK), buf(4, 2, HID, TOK), buf(NQ, PANEL, 2 * HC), buf(NQ, HC, PANEL),
            buf(2, PANEL, 2 * HC), buf(2, HC, PANEL),
            buf(2, 2, 2, PANEL, TOK), buf(2, 2, 2, 2, FEAT, TOK), buf(2, 4, 2, FEAT, TOK),
            buf(2, 2, FEAT, TOK), buf(2, 2, 2, FEAT, TOK),
            buf(2, 2, FEAT, TOK), buf(2, 2, FEAT, TOK),
            dma((2, 3)), dma((2, 3)), dma((2, 3)),
            dma((2, 2)), dma((2, 2)), dma((2, 4)), dma((2, 4)), dma((2, 4)), dma((2, 4)),
            dma((NQ, 6)), dma((NQ, 6)), dma((NQ, 4)), dma((NQ, 4)),
            dma((NQ, 6)), dma((NQ, 6)), dma((NQ, 4)), dma((NQ, 4)),
            dma((NQ, 2)), dma((NQ, 2)), dma((NQ, 2)), dma((NQ, 2)), dma((2,)), dma((2,)),
            dma((2, 2)), dma((2, 2)), dma((2, 6)), dma((2, 6)),
            dma((2, 2)), dma((2, 2)), dma((2, 2)), dma((2, 2)),
        ],
        name="layer",
        compiler_params=pltpu.CompilerParams(
            collective_id=0, has_side_effects=True, vmem_limit_bytes=60 * 2**20
        ),
    )(x_act[0].T, grad_out[0].T, w_gate, w_up, w_down)
    got, all_gu, all_dn = outs

    gu_block = pl.BlockSpec((1, PANEL, 2 * HC), lambda q: (q, 0, 0))
    dn_block = pl.BlockSpec((1, HC, PANEL), lambda q: (q, 0, 0))
    whole = pl.BlockSpec((FEAT, TOK), lambda q: (0, 0))
    *grads, out_t, dx_t = pl.pallas_call(
        widen_kernel,
        grid=(NQ,),
        out_shape=[
            shape((PANEL, HID), F32), shape((PANEL, HID), F32), shape((HID, PANEL), F32),
            shape((FEAT, TOK), BF16), shape((FEAT, TOK), BF16),
        ],
        in_specs=[
            gu_block, dn_block,
            pl.BlockSpec((2, 2, FEAT, TOK), lambda q: (0, 0, 0, 0)),
        ],
        out_specs=[
            pl.BlockSpec((PANEL, HC), lambda q: (0, q)),
            pl.BlockSpec((PANEL, HC), lambda q: (0, q)),
            pl.BlockSpec((HC, PANEL), lambda q: (q, 0)),
            whole, whole,
        ],
        name="widen",
        compiler_params=pltpu.CompilerParams(vmem_limit_bytes=60 * 2**20),
    )(all_gu, all_dn, got)
    return (out_t.T[None], dx_t.T[None], *grads)


def solution(mesh):
    acts = P("branch", "row", "col")
    return jax.shard_map(
        body,
        mesh=mesh,
        in_specs=(acts, acts, P("row", "col"), P("row", "col"), P("col", "row")),
        out_specs=(acts, acts, P("row", "col"), P("row", "col"), P("col", "row")),
        check_vma=False,
    )
```
